32 devices in a mesh: row: 4 (over x, core), col: 8 (over z, y).
Axes of the slice: x: 2, y: 2, z: 4, core: 2. Of those that a mesh axis runs over, the one named last changes fastest.
Arguments:
- inputs: bfloat16 [64, 128, 256], P('row', 'col'), may hold values from -6 to 6
- stored: bfloat16 [64, 128, 256], P('row', 'col'), may hold values from -6 to 6
- upstream: bfloat16 [64, 128, 256], P('row', 'col'), may hold values from -6 to 6
- weight_in: bfloat16 [256, 1024], replicated, may hold values from -0.375 to 0.375
- weight_out: bfloat16 [1024, 256], replicated, may hold values from -0.1875 to 0.1875
- kernel: bfloat16 [27, 27, 256], replicated, may hold values from -0.21875 to 0.21875
Outputs:
- grad_inputs: bfloat16 [64, 128, 256], P('row', 'col')
- grad_weight_in: bfloat16 [256, 1024], replicated
- grad_weight_out: bfloat16 [1024, 256], replicated
- grad_kernel: bfloat16 [27, 27, 256], replicated
The draws below stay inside these ranges and needn't reach their ends.
All inputs are finite; a program needn't handle non-finite values.
Results may differ from the reference program's by a relative error of at most 0.0052.
Values may be sent and summed in bfloat16 or wider, within the bound.
A program may use at most 64 MiB of HBM per device.

```python
import math
import jax
import jax.numpy as jnp
from jax import lax

C = 256
F = 1024
KS = 27
TH = 16
H = 64
W = 128
TOKENS = 8192


def level_of(rng, extent, split, low, largest):
    factor_of = 1.0
    for position, parts in split:
        draws = jax.random.uniform(jax.random.fold_in(jax.random.fold_in(rng, 6), position), (parts,), jnp.float32, low / len(split), largest / len(split))
        factor_of = factor_of * jnp.repeat(jnp.exp(draws), extent[position] // parts).reshape((-1,) + (1,) * (len(extent) - 1 - position))
    return factor_of


def normal_values(own_key, extent, deviation, limit, cuts=(), held_as=jnp.bfloat16):
    level = level_of(own_key, extent, cuts, -0.22, 0.18) if cuts else 1.0
    values = jax.random.normal(own_key, extent, jnp.float32) * deviation * level
    return jnp.minimum(jnp.maximum(values, -limit), limit).astype(held_as)


def setup_inputs(seed: int = 0) -> dict:
    arg_keys = jax.random.split(jax.random.key(seed), 7)
    return {
        "inputs": normal_values(arg_keys[0], (H, W, C), 1.0, 6.0, ((0, 4), (1, 8))),
        "stored": normal_values(arg_keys[1], (H, W, C), 1.0, 6.0, ((0, 4), (1, 8))),
        "upstream": normal_values(arg_keys[2], (H, W, C), 1.0, 6.0, ((0, 4), (1, 8))),
        "weight_in": normal_values(arg_keys[3], (C, F), C ** -0.5, 0.375),
        "weight_out": normal_values(arg_keys[4], (F, C), F ** -0.5, 0.1875),
        "kernel": normal_values(arg_keys[5], (KS, KS, C), (KS * KS) ** -0.5, 0.21875),
    }


gelu_coef = 0.044715
root_coef = math.sqrt(2.0 / math.pi)

def gelu_parts(values):
    tanh_part = jnp.tanh(root_coef * (values + gelu_coef * values * values * values))
    result = 0.5 * values * (1.0 + tanh_part)
    slopes = 0.5 * (1.0 + tanh_part) + 0.5 * values * (1.0 - tanh_part * tanh_part) * root_coef * (1.0 + 3.0 * gelu_coef * values * values)
    return (result, slopes)

def reference(inputs, stored, upstream, weight_in, weight_out, kernel):
    height, columns, channels = stored.shape
    hidden_units = weight_in.shape[1]
    blocks_z = stored.reshape(height // TH, TH * columns, channels)
    blocks_g = upstream.reshape(height // TH, TH * columns, channels)

    def block_step(state_pair, block_pair):
        stored_block, upstream_block = block_pair
        hidden = jnp.dot(stored_block, weight_in, preferred_element_type=jnp.float32)
        values, slopes = gelu_parts(hidden)
        active = values.astype(jnp.bfloat16)
        back_proj = jnp.dot(upstream_block, weight_out.T, preferred_element_type=jnp.float32)
        grad_hidden = (back_proj * slopes).astype(jnp.bfloat16)
        grad_mid = (upstream_block.astype(jnp.float32) + jnp.dot(grad_hidden, weight_in.T, preferred_element_type=jnp.float32)).astype(jnp.bfloat16)
        sum_in = state_pair[0] + jnp.dot(stored_block.T, grad_hidden, preferred_element_type=jnp.float32)
        sum_out = state_pair[1] + jnp.dot(active.T, upstream_block, preferred_element_type=jnp.float32)
        return ((sum_in, sum_out), grad_mid)
    start = (jnp.zeros((channels, hidden_units), jnp.float32), jnp.zeros((hidden_units, channels), jnp.float32))
    (sum_in, sum_out), mids = lax.scan(block_step, start, (blocks_z, blocks_g))
    grad_mid = mids.reshape(height, columns, channels)
    radius = KS // 2
    full_rows = height + KS - 1
    full_cols = columns + KS - 1
    grad_wide = grad_mid.astype(jnp.float32)
    grad_freq = jnp.fft.rfft2(grad_wide, s=(full_rows, full_cols), axes=(0, 1))
    kernel_freq = jnp.fft.rfft2(kernel.astype(jnp.float32), s=(full_rows, full_cols), axes=(0, 1))
    full_conv = jnp.fft.irfft2(grad_freq * kernel_freq, s=(full_rows, full_cols), axes=(0, 1))
    conv_back = full_conv[radius:radius + height, radius:radius + columns]
    grad_inputs = (grad_wide + conv_back).astype(jnp.bfloat16)
    input_freq = jnp.fft.rfft2(inputs.astype(jnp.float32), s=(full_rows, full_cols), axes=(0, 1))
    correlation = jnp.fft.irfft2(input_freq * jnp.conj(grad_freq), s=(full_rows, full_cols), axes=(0, 1))
    lagged = jnp.roll(correlation, (radius, radius), axis=(0, 1))
    back_k = lagged[:KS, :KS]
    grad_scale = 1.0 / math.sqrt(TOKENS)
    return (grad_inputs, (sum_in * grad_scale).astype(jnp.bfloat16), (sum_out * grad_scale).astype(jnp.bfloat16), (back_k * grad_scale).astype(jnp.bfloat16))
```

```python
import math

import jax
import jax.numpy as jnp
from jax import lax
from jax.experimental import pallas as pl
from jax.experimental.pallas import tpu as pltpu
from jax.sharding import PartitionSpec as P

KS = 27


gelu_coef = 0.044715
root_coef = math.sqrt(2.0 / math.pi)


def padded_2(block, sides, width):
    for axis, dim in sides:
        count = lax.axis_size(axis)
        forward = [(i, i + 1) for i in range(count - 1)]
        backward = [(target, source) for source, target in forward]
        low = lax.ppermute(
            lax.slice_in_dim(block, block.shape[dim] - width, None, axis=dim), axis, forward
        )
        high = lax.ppermute(lax.slice_in_dim(block, 0, width, axis=dim), axis, backward)
        block = jnp.concatenate([low, block, high], axis=dim)
    return block


def gelu_parts(values):
    tanh_part = jnp.tanh(root_coef * (values + gelu_coef * values * values * values))
    result = 0.5 * values * (1.0 + tanh_part)
    slopes = 0.5 * (1.0 + tanh_part) + 0.5 * values * (1.0 - tanh_part * tanh_part) * root_coef * (
        1.0 + 3.0 * gelu_coef * values * values
    )
    return (result, slopes)


def sweep_device(inputs, stored, upstream, weight_in, weight_out, kernel):
    tile_rows, tile_cols, channels = stored.shape
    radius = KS // 2
    flat_z = stored.reshape(tile_rows * tile_cols, channels)
    flat_g = upstream.reshape(tile_rows * tile_cols, channels)
    hidden = jnp.dot(flat_z, weight_in, preferred_element_type=jnp.float32)
    values, slopes = gelu_parts(hidden)
    active = values.astype(jnp.bfloat16)
    back_proj = jnp.einsum("nc,fc->nf", flat_g, weight_out, preferred_element_type=jnp.float32)
    grad_hidden = (back_proj * slopes).astype(jnp.bfloat16)
    grad_flat = (
        flat_g.astype(jnp.float32)
        + jnp.einsum("nf,cf->nc", grad_hidden, weight_in, preferred_element_type=jnp.float32)
    ).astype(jnp.bfloat16)
    sum_in = jnp.einsum("nc,nf->cf", flat_z, grad_hidden, preferred_element_type=jnp.float32)
    sum_out = jnp.einsum("nf,nc->fc", active, flat_g, preferred_element_type=jnp.float32)
    grad_mid = grad_flat.reshape(tile_rows, tile_cols, channels)
    padded = padded_2(grad_mid, (("row", 0), ("col", 1)), radius)
    kernel_wide = kernel.astype(jnp.float32)

    def sweep(row_off, state_pair):
        accumulated, kernel_sums = state_pair
        slab_rows = lax.dynamic_slice_in_dim(padded, 2 * radius - row_off, tile_rows, 0)
        tap_row = lax.dynamic_index_in_dim(kernel_wide, row_off, 0, keepdims=False)
        tap_sums = []
        for offset in range(KS):
            shifted = slab_rows[:, 2 * radius - offset : 2 * radius - offset + tile_cols].astype(
                jnp.float32
            )
            accumulated = accumulated + tap_row[offset] * shifted
            tap_sums.append(jnp.sum(inputs.astype(jnp.float32) * shifted, axis=(0, 1)))
        kernel_sums = lax.dynamic_update_index_in_dim(kernel_sums, jnp.stack(tap_sums), row_off, 0)
        return (accumulated, kernel_sums)

    start = (
        jnp.zeros((tile_rows, tile_cols, channels), jnp.float32),
        jnp.zeros((KS, KS, channels), jnp.float32),
    )
    accumulated, kernel_sums = lax.fori_loop(0, KS, sweep, start)
    grad_inputs = (grad_mid.astype(jnp.float32) + accumulated).astype(jnp.bfloat16)
    devices_all = lax.axis_size("row") * lax.axis_size("col")
    pixel_count = tile_rows * tile_cols * devices_all
    grad_scale = 1.0 / math.sqrt(pixel_count)
    total_in, total_out, total_kernel = lax.psum((sum_in, sum_out, kernel_sums), ("row", "col"))
    final_in = (total_in * grad_scale).astype(jnp.bfloat16)
    final_out = (total_out * grad_scale).astype(jnp.bfloat16)
    final_kernel = (total_kernel * grad_scale).astype(jnp.bfloat16)
    return (grad_inputs, final_in, final_out, final_kernel)


MESH = pl.DeviceIdType.MESH
LANE = 128
SUB = 8


def round_up(value, unit):
    return -(-value // unit) * unit


def dot(a, b, over_a, over_b):
    return lax.dot_general(
        a, b, (((over_a,), (over_b,)), ((), ())), preferred_element_type=jnp.float32
    )


def roll_left(v, shift, axis):
    size = v.shape[axis]
    shift = shift % size
    return v if shift == 0 else pltpu.roll(v, size - shift, axis)


def moved(v, rows, cols, d_row, d_col):
    tile = lax.broadcasted_iota(jnp.int32, v.shape, 0)
    row, col = tile // cols + d_row, tile % cols + d_col
    inside = (row >= 0) & (row < rows) & (col >= 0) & (col < cols)
    return jnp.where(inside, roll_left(v, d_row * cols + d_col, 0), 0.0)


def bytes_of(ref, sem):
    pltpu.make_async_copy(ref, ref, sem).wait()


def fused_kernel(
    rows, cols, tile_cols, radius, scale,
    x_ref, z_ref, g_ref, wi_ref, wo_ref, k_ref,
    gi_ref, gwi_ref, gwo_ref, gk_ref,
    x_send, x_recv, g_send, g_recv, o_send, o_recv,
    part, l1, half, l2, allq, gk_send, gk_recv,
    wide, x3, g3, o3, taps, taps_t, skew, folded, bands, k_mat, m_mat, x_sh, gk_t,
    ssem, rsem,
):
    n = rows * cols
    pixels, channels = z_ref.shape
    own = channels // n
    side = k_ref.shape[0]
    lead = pixels - tile_cols * radius - tile_cols
    width = skew.shape[2]
    span = 3 * pixels
    per_block = LANE // tile_cols
    chunks = pixels // tile_cols
    my_row, my_col = lax.axis_index("row"), lax.axis_index("col")
    me = my_row * cols + my_col
    f32, bf16 = jnp.float32, jnp.bfloat16

    def send(src, dst, phase, row, col):
        pltpu.make_async_remote_copy(
            src_ref=src, dst_ref=dst, send_sem=ssem.at[phase], recv_sem=rsem.at[phase],
            device_id=(row, col), device_id_type=MESH,
        ).start()

    def to_all(fn):
        @pl.loop(1, n)
        def _(p):
            target = lax.rem(me + p, n)
            fn(target, target // cols, lax.rem(target, cols))

    barrier = pltpu.get_barrier_semaphore()
    to_all(lambda t, r, c: pl.semaphore_signal(
        barrier, inc=1, device_id=(r, c), device_id_type=MESH))

    x_send[...] = x_ref[...].astype(f32).T.reshape(n, own, pixels).astype(bf16)
    x_recv[pl.ds(me, 1)] = x_send[pl.ds(me, 1)]
    pl.semaphore_wait(barrier, n - 1)
    to_all(lambda t, r, c: send(x_send.at[t], x_recv.at[me], 0, r, c))

    z, g = z_ref[...], g_ref[...]
    total = g.astype(f32)
    block = wi_ref.shape[1] // rows
    for f in range(rows):
        w_in = wi_ref[:, f * block:(f + 1) * block]
        w_out = wo_ref[f * block:(f + 1) * block, :]
        values, slopes = gelu_parts(dot(z, w_in, 1, 0))
        active = values.astype(bf16)
        grad_hidden = (dot(g, w_out, 1, 1) * slopes).astype(bf16)
        total = total + dot(grad_hidden, w_in, 1, 1)
        part[f, :channels] = dot(z, grad_hidden, 0, 0).astype(bf16)
        part[f, channels:] = dot(active, g, 0, 0).astype(bf16)
    g_send[...] = total.T.reshape(n, own, pixels).astype(bf16)
    g_recv[pl.ds(me, 1)] = g_send[pl.ds(me, 1)]
    to_all(lambda t, r, c: send(g_send.at[t], g_recv.at[me], 1, r, c))
    for p in range(1, rows):
        r = lax.rem(my_row + p, rows)
        send(part.at[r], l1.at[my_row], 2, r, my_col)
    l1[pl.ds(my_row, 1)] = part[pl.ds(my_row, 1)]

    taps[...] = jnp.zeros_like(taps)
    for a in range(side):
        tap = k_ref[a].astype(f32)
        at = lead + tile_cols * a
        taps[0, at:at + radius + 1, :] = tap[radius:]
        taps[1, at + tile_cols - radius:at + tile_cols, :] = tap[:radius]
    lanes_at = pl.multiple_of(me * own // LANE * LANE, LANE)
    for sign in range(2):
        taps_t[...] = taps[sign, :, pl.ds(lanes_at, LANE)].T
        line = taps_t[pl.ds(pl.multiple_of(lax.rem(me * own, LANE), SUB), own), :]
        for t in range(SUB):
            skew[sign * own:(sign + 1) * own, t, :] = pltpu.roll(line, t, 1) if t else line

    at_or_after = (
        lax.broadcasted_iota(jnp.int32, (tile_cols, span), 1) % tile_cols
        >= lax.broadcasted_iota(jnp.int32, (tile_cols, span), 0)
    )
    offsets = (-1, 0, 1)

    bytes_of(x_recv.at[pl.ds(0, n - 1)], rsem.at[0])
    wide[...] = x_recv[...].astype(f32)
    for c in range(own):
        x3[c] = wide[:, c, :]
    bytes_of(g_recv.at[pl.ds(0, n - 1)], rsem.at[1])
    wide[...] = g_recv[...].astype(f32)
    for c in range(own):
        g3[c] = wide[:, c, :]

    @pl.loop(0, own)
    def _(c):
        here = x3[c]
        for i, d_col in enumerate(offsets):
            for j, d_row in enumerate(offsets):
                at = i * span + j * pixels
                x_sh[:, at:at + pixels] = moved(here, rows, cols, d_row, d_col).astype(bf16)
        m_mat[...] = dot(g3[c].astype(bf16), x_sh[...], 0, 0)

        def piece(q, i):
            return m_mat[q * tile_cols:(q + 1) * tile_cols, i * span:(i + 1) * span]

        def lagged(q, sign):
            after, before = ((1, 2), (0, 1))[sign]
            out = jnp.zeros((tile_cols, span), f32)
            if q >= 1:
                out = jnp.where(at_or_after, piece(q - 1, after), 0.0)
            if q < chunks:
                out = out + jnp.where(at_or_after, 0.0, piece(q, before))
            return out

        for sign in range(2):
            parts = []
            for i in range(per_block):
                v = jnp.zeros((tile_cols, width), f32)
                for q in range(i, chunks + 1, per_block):
                    skip = q // per_block * LANE
                    piece_q = lagged(q, sign)[:, skip:skip + width]
                    missing = width - piece_q.shape[1]
                    if missing:
                        piece_q = jnp.concatenate(
                            [piece_q, jnp.zeros((tile_cols, missing), f32)], axis=1)
                    v = v + piece_q
                parts.append(v)
            while len(parts) > 1:
                m = len(parts) // 2
                parts = [parts[i] + roll_left(parts[i + m], m * tile_cols, 1) for i in range(m)]
            v = parts[0]
            m = tile_cols // 2
            while m >= SUB:
                v = v[:m] + roll_left(v[m:], m, 1)
                m //= 2
            folded[sign * own + c] = v

    lines = folded[:, 0, :]
    for t in range(1, SUB):
        lines = lines + roll_left(folded[:, t, :], t, 1)
    keep = gk_send.shape[1] // 2
    lines = (lines * scale)[:, :keep]
    gk_send[...] = jnp.concatenate([lines[:own], lines[own:]], axis=1).astype(bf16)
    gk_recv[pl.ds(me, 1)] = gk_send[...][None]
    to_all(lambda t, r, c: send(gk_send, gk_recv.at[me], 6, r, c))

    bytes_of(l1.at[pl.ds(0, rows - 1)], rsem.at[2])
    for j in range(cols):
        size = half.shape[1]
        v = l1[0, j * size:(j + 1) * size, :].astype(f32)
        for r in range(1, rows):
            v = v + l1[r, j * size:(j + 1) * size, :].astype(f32)
        half[j] = v.astype(bf16)
    for p in range(1, cols):
        c = lax.rem(my_col + p, cols)
        send(half.at[c], l2.at[my_col], 3, my_row, c)
    l2[pl.ds(my_col, 1)] = half[pl.ds(my_col, 1)]

    bands[...] = jnp.zeros_like(bands)
    @pl.loop(0, own)
    def _(c):
        for sign in range(2):
            v = skew[sign * own + c]
            m = SUB
            while m < tile_cols:
                v = jnp.concatenate([v, pltpu.roll(v, m, 1)], axis=0)
                m *= 2
            parts = [v]
            while len(parts) < per_block:
                m = len(parts) * tile_cols
                parts = parts + [pltpu.roll(u, m, 1) for u in parts]
            for i, u in enumerate(parts):
                bands[sign, i * tile_cols:(i + 1) * tile_cols, pixels:pixels + width] = u

        def band(q, sign):
            at = q % per_block * tile_cols
            skip = pixels - q // per_block * LANE
            return bands[sign, at:at + tile_cols, skip:skip + span]

        for q in range(chunks):
            at = slice(q * tile_cols, (q + 1) * tile_cols)
            k_mat[at, :span] = jnp.where(at_or_after, band(q + 1, 1), 0.0).astype(bf16)
            k_mat[at, span:2 * span] = jnp.where(
                at_or_after, band(q + 1, 0), band(q, 1)).astype(bf16)
            k_mat[at, 2 * span:] = jnp.where(at_or_after, 0.0, band(q, 0)).astype(bf16)
        here = g3[c]
        spread = dot(here.astype(bf16), k_mat[...], 1, 0)
        result = here
        for i, d_col in enumerate(offsets):
            for j, d_row in enumerate(offsets):
                at = i * span + j * pixels
                result = result + moved(spread[:, at:at + pixels], rows, cols, -d_row, -d_col)
        o3[c] = result

    for c in range(own):
        wide[:, c, :] = o3[c]
    o_send[...] = wide[...].astype(bf16)
    o_recv[pl.ds(me, 1)] = o_send[pl.ds(me, 1)]
    to_all(lambda t, r, c: send(o_send.at[t], o_recv.at[me], 7, r, c))

    bytes_of(l2.at[pl.ds(0, cols - 1)], rsem.at[3])
    v = l2[0].astype(f32)
    for c in range(1, cols):
        v = v + l2[c].astype(f32)
    mine = allq.at[my_row, my_col]
    mine[...] = (v * scale).astype(bf16)
    for p in range(1, cols):
        send(mine, mine, 4, my_row, lax.rem(my_col + p, cols))

    bytes_of(allq.at[0, pl.ds(0, cols - 1)], rsem.at[4])
    for p in range(1, rows):
        send(allq.at[my_row], allq.at[my_row], 5, lax.rem(my_row + p, rows), my_col)

    bytes_of(o_recv.at[pl.ds(0, n - 1)], rsem.at[7])
    gi_ref[...] = o_recv[...].astype(f32).reshape(channels, pixels).T.astype(bf16)

    bytes_of(gk_recv.at[pl.ds(0, n - 1)], rsem.at[6])
    gk_t[...] = gk_recv[...].astype(f32).reshape(channels, 2 * keep).T
    for a in range(side):
        at = lead + tile_cols * a
        low = gk_t[keep + at + tile_cols - radius:keep + at + tile_cols, :]
        high = gk_t[at:at + radius + 1, :]
        gk_ref[a] = jnp.concatenate([low, high], axis=0).astype(bf16)

    bytes_of(allq.at[pl.ds(0, rows - 1)], rsem.at[5])
    per_half = cols // 2
    for f in range(rows):
        at = slice(f * block, (f + 1) * block)
        gwi_ref[:, at] = allq[f, :per_half].reshape(channels, block)
        gwo_ref[at, :] = allq[f, per_half:].reshape(block, channels)

    bytes_of(x_send.at[pl.ds(0, n - 1)], ssem.at[0])
    bytes_of(g_send.at[pl.ds(0, n - 1)], ssem.at[1])
    bytes_of(part.at[pl.ds(0, rows - 1)], ssem.at[2])
    bytes_of(half.at[pl.ds(0, cols - 1)], ssem.at[3])
    bytes_of(l2.at[pl.ds(0, cols - 1)], ssem.at[4])
    bytes_of(allq.at[pl.ds(0, rows - 1)], ssem.at[5])
    bytes_of(gk_recv.at[pl.ds(0, n - 1)], ssem.at[6])
    bytes_of(o_send.at[pl.ds(0, n - 1)], ssem.at[7])


def fits(rows, cols, tile_rows, tile_cols, channels, hidden):
    n = rows * cols
    pixels = tile_rows * tile_cols
    radius = KS // 2
    return (
        channels % n == 0
        and channels // n == SUB
        and channels % LANE == 0
        and rows > 1
        and cols % 2 == 0
        and hidden == rows * channels
        and pixels == 2 * LANE
        and tile_cols == 2 * SUB
        and radius < min(tile_rows, tile_cols)
        and (2 * channels) % (cols * 2 * SUB) == 0
    )


def fused_device(inputs, stored, upstream, weight_in, weight_out, kernel):
    rows, cols = lax.axis_size("row"), lax.axis_size("col")
    tile_rows, tile_cols, channels = stored.shape
    n, pixels, hidden = rows * cols, tile_rows * tile_cols, weight_in.shape[1]
    side = kernel.shape[0]
    radius = side // 2
    own = channels // n
    taps = pixels - tile_cols * radius - tile_cols + tile_cols * side
    width = round_up(taps + LANE - 1, LANE)
    keep = round_up(taps, LANE)
    span = 3 * pixels
    scale = 1.0 / math.sqrt(pixels * n)
    bf16, f32 = jnp.bfloat16, jnp.float32
    flat = (pixels, channels)
    piece = 2 * channels // cols
    vmem = pl.BlockSpec(memory_space=pltpu.VMEM)
    results = pl.pallas_call(
        lambda *refs: fused_kernel(rows, cols, tile_cols, radius, scale, *refs),
        out_shape=(
            jax.ShapeDtypeStruct(flat, bf16),
            jax.ShapeDtypeStruct(weight_in.shape, bf16),
            jax.ShapeDtypeStruct(weight_out.shape, bf16),
            jax.ShapeDtypeStruct(kernel.shape, bf16),
        ),
        in_specs=[vmem] * 6,
        out_specs=(vmem,) * 4,
        scratch_shapes=[pltpu.VMEM((n, own, pixels), bf16)] * 6 + [
            pltpu.VMEM((rows, 2 * channels, channels), bf16),
            pltpu.VMEM((rows, 2 * channels, channels), bf16),
            pltpu.VMEM((cols, piece, channels), bf16),
            pltpu.VMEM((cols, piece, channels), bf16),
            pltpu.VMEM((rows, cols, piece, channels), bf16),
            pltpu.VMEM((own, 2 * keep), bf16),
            pltpu.VMEM((n, own, 2 * keep), bf16),
            pltpu.VMEM((n, own, pixels), f32),
            pltpu.VMEM((own, n, pixels), f32),
            pltpu.VMEM((own, n, pixels), f32),
            pltpu.VMEM((own, n, pixels), f32),
            pltpu.VMEM((2, width, channels), f32),
            pltpu.VMEM((LANE, width), f32),
            pltpu.VMEM((2 * own, SUB, width), f32),
            pltpu.VMEM((2 * own, SUB, width), f32),
            pltpu.VMEM((2, LANE, pixels + span), f32),
            pltpu.VMEM((pixels, 3 * span), bf16),
            pltpu.VMEM((pixels, 3 * span), f32),
            pltpu.VMEM((n, 3 * span), bf16),
            pltpu.VMEM((2 * keep, channels), f32),
            pltpu.SemaphoreType.DMA((8,)),
            pltpu.SemaphoreType.DMA((8,)),
        ],
        compiler_params=pltpu.CompilerParams(
            collective_id=0, has_side_effects=True, vmem_limit_bytes=48 * 1024 * 1024
        ),
    )(
        inputs.reshape(flat), stored.reshape(flat), upstream.reshape(flat),
        weight_in, weight_out, kernel,
    )
    return (results[0].reshape(stored.shape), *results[1:])


def per_device(inputs, stored, upstream, weight_in, weight_out, kernel):
    args = (inputs, stored, upstream, weight_in, weight_out, kernel)
    sizes = (lax.axis_size("row"), lax.axis_size("col"))
    if fits(*sizes, *stored.shape, weight_in.shape[1]):
        return fused_device(*args)
    return sweep_device(*args)


def solution(mesh):
    return jax.shard_map(
        per_device,
        mesh=mesh,
        in_specs=(
            P("row", "col", None),
            P("row", "col", None),
            P("row", "col", None),
            P(),
            P(),
            P(),
        ),
        out_specs=(P("row", "col", None), P(), P(), P()),
        check_vma=False,
    )
```

```python
import math

import jax
import jax.numpy as jnp
from jax import lax
from jax.experimental import pallas as pl
from jax.experimental.pallas import tpu as pltpu
from jax.sharding import PartitionSpec as P

KS = 27


gelu_coef = 0.044715
root_coef = math.sqrt(2.0 / math.pi)


def padded_2(block, sides, width):
    for axis, dim in sides:
        count = lax.axis_size(axis)
        forward = [(i, i + 1) for i in range(count - 1)]
        backward = [(target, source) for source, target in forward]
        low = lax.ppermute(
            lax.slice_in_dim(block, block.shape[dim] - width, None, axis=dim), axis, forward
        )
        high = lax.ppermute(lax.slice_in_dim(block, 0, width, axis=dim), axis, backward)
        block = jnp.concatenate([low, block, high], axis=dim)
    return block


def gelu_parts(values):
    tanh_part = jnp.tanh(root_coef * (values + gelu_coef * values * values * values))
    result = 0.5 * values * (1.0 + tanh_part)
    slopes = 0.5 * (1.0 + tanh_part) + 0.5 * values * (1.0 - tanh_part * tanh_part) * root_coef * (
        1.0 + 3.0 * gelu_coef * values * values
    )
    return (result, slopes)


def sweep_device(inputs, stored, upstream, weight_in, weight_out, kernel):
    tile_rows, tile_cols, channels = stored.shape
    radius = KS // 2
    flat_z = stored.reshape(tile_rows * tile_cols, channels)
    flat_g = upstream.reshape(tile_rows * tile_cols, channels)
    hidden = jnp.dot(flat_z, weight_in, preferred_element_type=jnp.float32)
    values, slopes = gelu_parts(hidden)
    active = values.astype(jnp.bfloat16)
    back_proj = jnp.einsum("nc,fc->nf", flat_g, weight_out, preferred_element_type=jnp.float32)
    grad_hidden = (back_proj * slopes).astype(jnp.bfloat16)
    grad_flat = (
        flat_g.astype(jnp.float32)
        + jnp.einsum("nf,cf->nc", grad_hidden, weight_in, preferred_element_type=jnp.float32)
    ).astype(jnp.bfloat16)
    sum_in = jnp.einsum("nc,nf->cf", flat_z, grad_hidden, preferred_element_type=jnp.float32)
    sum_out = jnp.einsum("nf,nc->fc", active, flat_g, preferred_element_type=jnp.float32)
    grad_mid = grad_flat.reshape(tile_rows, tile_cols, channels)
    padded = padded_2(grad_mid, (("row", 0), ("col", 1)), radius)
    kernel_wide = kernel.astype(jnp.float32)

    def sweep(row_off, state_pair):
        accumulated, kernel_sums = state_pair
        slab_rows = lax.dynamic_slice_in_dim(padded, 2 * radius - row_off, tile_rows, 0)
        tap_row = lax.dynamic_index_in_dim(kernel_wide, row_off, 0, keepdims=False)
        tap_sums = []
        for offset in range(KS):
            shifted = slab_rows[:, 2 * radius - offset : 2 * radius - offset + tile_cols].astype(
                jnp.float32
            )
            accumulated = accumulated + tap_row[offset] * shifted
            tap_sums.append(jnp.sum(inputs.astype(jnp.float32) * shifted, axis=(0, 1)))
        kernel_sums = lax.dynamic_update_index_in_dim(kernel_sums, jnp.stack(tap_sums), row_off, 0)
        return (accumulated, kernel_sums)

    start = (
        jnp.zeros((tile_rows, tile_cols, channels), jnp.float32),
        jnp.zeros((KS, KS, channels), jnp.float32),
    )
    accumulated, kernel_sums = lax.fori_loop(0, KS, sweep, start)
    grad_inputs = (grad_mid.astype(jnp.float32) + accumulated).astype(jnp.bfloat16)
    devices_all = lax.axis_size("row") * lax.axis_size("col")
    pixel_count = tile_rows * tile_cols * devices_all
    grad_scale = 1.0 / math.sqrt(pixel_count)
    total_in, total_out, total_kernel = lax.psum((sum_in, sum_out, kernel_sums), ("row", "col"))
    final_in = (total_in * grad_scale).astype(jnp.bfloat16)
    final_out = (total_out * grad_scale).astype(jnp.bfloat16)
    final_kernel = (total_kernel * grad_scale).astype(jnp.bfloat16)
    return (grad_inputs, final_in, final_out, final_kernel)


MESH = pl.DeviceIdType.MESH
LANE = 128
SUB = 8


def round_up(value, unit):
    return -(-value // unit) * unit


def dot(a, b, over_a, over_b):
    return lax.dot_general(
        a, b, (((over_a,), (over_b,)), ((), ())), preferred_element_type=jnp.float32
    )


def roll_left(v, shift, axis):
    size = v.shape[axis]
    shift = shift % size
    return v if shift == 0 else pltpu.roll(v, size - shift, axis)


def moved(v, rows, cols, d_row, d_col):
    tile = lax.broadcasted_iota(jnp.int32, v.shape, 0)
    row, col = tile // cols + d_row, tile % cols + d_col
    inside = (row >= 0) & (row < rows) & (col >= 0) & (col < cols)
    return jnp.where(inside, roll_left(v, d_row * cols + d_col, 0), 0.0)


def bytes_of(ref, sem):
    pltpu.make_async_copy(ref, ref, sem).wait()


def fused_kernel(
    rows, cols, tile_cols, radius, scale,
    x_hbm, z_hbm, g_hbm, wi_hbm, wo_hbm, k_hbm,
    gi_ref, gwi_ref, gwo_ref, gk_ref,
    x_ref, z_ref, g_ref, wi_ref, wo_ref, k_ref,
    x_send, x_recv, g_send, g_recv, o_send, o_recv,
    part, from_pair, paired, from_rows, half, from_cols, allq, gk_send, gk_recv,
    wide, x3, g3, o3, taps, taps_t, skew, folded, bands, k_mat, m_mat, x_sh, gk_t,
    isem, ssem, rsem,
):
    n = rows * cols
    pixels, channels = z_ref.shape
    own = channels // n
    side = k_ref.shape[0]
    lead = pixels - tile_cols * radius - tile_cols
    width = skew.shape[2]
    span = 3 * pixels
    per_block = LANE // tile_cols
    chunks = pixels // tile_cols
    my_row, my_col = lax.axis_index("row"), lax.axis_index("col")
    me = my_row * cols + my_col
    pairs = rows // 2
    my_pair, core = my_row // 2, lax.rem(my_row, 2)
    other = 1 - core
    f32, bf16 = jnp.float32, jnp.bfloat16

    def send(src, dst, phase, row, col):
        pltpu.make_async_remote_copy(
            src_ref=src, dst_ref=dst, send_sem=ssem.at[phase], recv_sem=rsem.at[phase],
            device_id=(row, col), device_id_type=MESH,
        ).start()

    def sum_pair(s):
        bytes_of(from_pair.at[s], rsem.at[4 + s])
        for p in range(pairs):
            paired[s, p] = (
                part[s, core, p].astype(f32) + from_pair[s, p].astype(f32)).astype(bf16)
        for p in range(1, pairs):
            to = lax.rem(my_pair + p, pairs)
            send(paired.at[s, to], from_rows.at[s, my_pair], 6 + s, 2 * to + core, my_col)
        from_rows[s, pl.ds(my_pair, 1)] = paired[s, pl.ds(my_pair, 1)]

    def sum_rows(s):
        bytes_of(from_rows.at[s, pl.ds(0, pairs - 1)], rsem.at[6 + s])
        v = from_rows[s, 0].astype(f32)
        for p in range(1, pairs):
            v = v + from_rows[s, p].astype(f32)
        half[s] = v.reshape(half.shape[1:]).astype(bf16)
        for p in range(1, cols):
            c = lax.rem(my_col + p, cols)
            send(half.at[s, c], from_cols.at[s, my_col], 8 + s, my_row, c)
        from_cols[s, pl.ds(my_col, 1)] = half[s, pl.ds(my_col, 1)]

    def sum_cols(s):
        bytes_of(from_cols.at[s, pl.ds(0, cols - 1)], rsem.at[8 + s])
        v = from_cols[s, 0].astype(f32)
        for c in range(1, cols):
            v = v + from_cols[s, c].astype(f32)
        mine = allq.at[s, core, my_pair, my_col]
        mine[...] = (v * scale).astype(bf16)
        for p in range(1, cols):
            send(mine, mine, 10 + s, my_row, lax.rem(my_col + p, cols))

    def share_rows(s):
        bytes_of(allq.at[s, 0, 0, pl.ds(0, cols - 1)], rsem.at[10 + s])
        mine = allq.at[s, core, my_pair]
        for p in range(1, pairs):
            to = lax.rem(my_pair + p, pairs)
            send(mine, mine, 12 + s, 2 * to + core, my_col)

    def share_pair(s):
        bytes_of(allq.at[s, 0, pl.ds(0, pairs - 1)], rsem.at[12 + s])
        mine = allq.at[s, core]
        send(mine, mine, 14 + s, my_row + other - core, my_col)

    def to_all(fn):
        @pl.loop(1, n)
        def _(p):
            target = lax.rem(me + p, n)
            fn(target, target // cols, lax.rem(target, cols))

    loads = [
        pltpu.make_async_copy(source, target, isem.at[i])
        for i, (source, target) in enumerate((
            (x_hbm, x_ref), (z_hbm, z_ref), (g_hbm, g_ref),
            (wi_hbm, wi_ref), (wo_hbm, wo_ref), (k_hbm, k_ref),
        ))
    ]
    for load in loads:
        load.start()
    barrier = pltpu.get_barrier_semaphore()
    to_all(lambda t, r, c: pl.semaphore_signal(
        barrier, inc=1, device_id=(r, c), device_id_type=MESH))

    loads[0].wait()
    x_send[...] = x_ref[...].astype(f32).T.reshape(n, own, pixels).astype(bf16)
    x_recv[pl.ds(me, 1)] = x_send[pl.ds(me, 1)]
    pl.semaphore_wait(barrier, n - 1)
    to_all(lambda t, r, c: send(x_send.at[t], x_recv.at[me], 0, r, c))

    for load in loads[1:]:
        load.wait()
    z, g = z_ref[...], g_ref[...]
    total = g.astype(f32)
    block = wi_ref.shape[1] // rows
    for f in range(rows):
        w_in = wi_ref[:, f * block:(f + 1) * block]
        w_out = wo_ref[f * block:(f + 1) * block, :]
        values, slopes = gelu_parts(dot(z, w_in, 1, 0))
        active = values.astype(bf16)
        grad_hidden = (dot(g, w_out, 1, 1) * slopes).astype(bf16)
        total = total + dot(grad_hidden, w_in, 1, 1)
        part[0, f % 2, f // 2] = dot(z, grad_hidden, 0, 0).astype(bf16)
        part[1, f % 2, f // 2] = dot(active, g, 0, 0).astype(bf16)
    g_send[...] = total.T.reshape(n, own, pixels).astype(bf16)
    g_recv[pl.ds(me, 1)] = g_send[pl.ds(me, 1)]
    to_all(lambda t, r, c: send(g_send.at[t], g_recv.at[me], 1, r, c))
    for s in range(2):
        send(part.at[s, other], from_pair.at[s], 4 + s, my_row + other - core, my_col)

    taps[...] = jnp.zeros_like(taps)
    for a in range(side):
        tap = k_ref[a].astype(f32)
        at = lead + tile_cols * a
        taps[0, at:at + radius + 1, :] = tap[radius:]
        taps[1, at + tile_cols - radius:at + tile_cols, :] = tap[:radius]
    lanes_at = pl.multiple_of(me * own // LANE * LANE, LANE)
    for sign in range(2):
        taps_t[...] = taps[sign, :, pl.ds(lanes_at, LANE)].T
        line = taps_t[pl.ds(pl.multiple_of(lax.rem(me * own, LANE), SUB), own), :]
        for t in range(SUB):
            skew[sign * own:(sign + 1) * own, t, :] = pltpu.roll(line, t, 1) if t else line

    at_or_after = (
        lax.broadcasted_iota(jnp.int32, (tile_cols, span), 1) % tile_cols
        >= lax.broadcasted_iota(jnp.int32, (tile_cols, span), 0)
    )
    offsets = (-1, 0, 1)

    sum_pair(0)
    sum_pair(1)
    bytes_of(x_recv.at[pl.ds(0, n - 1)], rsem.at[0])
    wide[...] = x_recv[...].astype(f32)
    for c in range(own):
        x3[c] = wide[:, c, :]
    bytes_of(g_recv.at[pl.ds(0, n - 1)], rsem.at[1])
    wide[...] = g_recv[...].astype(f32)
    for c in range(own):
        g3[c] = wide[:, c, :]

    def correlate(c):
        here = x3[c]
        for i, d_col in enumerate(offsets):
            for j, d_row in enumerate(offsets):
                at = i * span + j * pixels
                x_sh[:, at:at + pixels] = moved(here, rows, cols, d_row, d_col).astype(bf16)
        m_mat[...] = dot(g3[c].astype(bf16), x_sh[...], 0, 0)

        def piece(q, i):
            return m_mat[q * tile_cols:(q + 1) * tile_cols, i * span:(i + 1) * span]

        def lagged(q, sign):
            after, before = ((1, 2), (0, 1))[sign]
            out = jnp.zeros((tile_cols, span), f32)
            if q >= 1:
                out = jnp.where(at_or_after, piece(q - 1, after), 0.0)
            if q < chunks:
                out = out + jnp.where(at_or_after, 0.0, piece(q, before))
            return out

        for sign in range(2):
            parts = []
            for i in range(per_block):
                v = jnp.zeros((tile_cols, width), f32)
                for q in range(i, chunks + 1, per_block):
                    skip = q // per_block * LANE
                    piece_q = lagged(q, sign)[:, skip:skip + width]
                    missing = width - piece_q.shape[1]
                    if missing:
                        piece_q = jnp.concatenate(
                            [piece_q, jnp.zeros((tile_cols, missing), f32)], axis=1)
                    v = v + piece_q
                parts.append(v)
            while len(parts) > 1:
                m = len(parts) // 2
                parts = [parts[i] + roll_left(parts[i + m], m * tile_cols, 1) for i in range(m)]
            v = parts[0]
            m = tile_cols // 2
            while m >= SUB:
                v = v[:m] + roll_left(v[m:], m, 1)
                m //= 2
            folded[sign * own + c] = v

    pl.loop(0, own // 2)(correlate)
    sum_rows(0)
    sum_rows(1)
    pl.loop(own // 2, own)(correlate)

    lines = folded[:, 0, :]
    for t in range(1, SUB):
        lines = lines + roll_left(folded[:, t, :], t, 1)
    keep = gk_send.shape[1] // 2
    lines = (lines * scale)[:, :keep]
    gk_send[...] = jnp.concatenate([lines[:own], lines[own:]], axis=1).astype(bf16)
    gk_recv[pl.ds(me, 1)] = gk_send[...][None]
    to_all(lambda t, r, c: send(gk_send, gk_recv.at[me], 2, r, c))

    sum_cols(0)
    sum_cols(1)

    bands[...] = jnp.zeros_like(bands)

    def convolve(c):
        for sign in range(2):
            v = skew[sign * own + c]
            m = SUB
            while m < tile_cols:
                v = jnp.concatenate([v, pltpu.roll(v, m, 1)], axis=0)
                m *= 2
            parts = [v]
            while len(parts) < per_block:
                m = len(parts) * tile_cols
                parts = parts + [pltpu.roll(u, m, 1) for u in parts]
            for i, u in enumerate(parts):
                bands[sign, i * tile_cols:(i + 1) * tile_cols, pixels:pixels + width] = u

        def band(q, sign):
            at = q % per_block * tile_cols
            skip = pixels - q // per_block * LANE
            return bands[sign, at:at + tile_cols, skip:skip + span]

        for q in range(chunks):
            at = slice(q * tile_cols, (q + 1) * tile_cols)
            k_mat[at, :span] = jnp.where(at_or_after, band(q + 1, 1), 0.0).astype(bf16)
            k_mat[at, span:2 * span] = jnp.where(
                at_or_after, band(q + 1, 0), band(q, 1)).astype(bf16)
            k_mat[at, 2 * span:] = jnp.where(at_or_after, 0.0, band(q, 0)).astype(bf16)
        here = g3[c]
        spread = dot(here.astype(bf16), k_mat[...], 1, 0)
        result = here
        for i, d_col in enumerate(offsets):
            for j, d_row in enumerate(offsets):
                at = i * span + j * pixels
                result = result + moved(spread[:, at:at + pixels], rows, cols, -d_row, -d_col)
        o3[c] = result

    pl.loop(0, own // 2)(convolve)
    share_rows(0)
    share_rows(1)
    pl.loop(own // 2, own)(convolve)

    for c in range(own):
        wide[:, c, :] = o3[c]
    o_send[...] = wide[...].astype(bf16)
    o_recv[pl.ds(me, 1)] = o_send[pl.ds(me, 1)]
    to_all(lambda t, r, c: send(o_send.at[t], o_recv.at[me], 3, r, c))

    share_pair(0)
    share_pair(1)

    bytes_of(o_recv.at[pl.ds(0, n - 1)], rsem.at[3])
    gi_ref[...] = o_recv[...].astype(f32).reshape(channels, pixels).T.astype(bf16)

    bytes_of(gk_recv.at[pl.ds(0, n - 1)], rsem.at[2])
    gk_t[...] = gk_recv[...].astype(f32).reshape(channels, 2 * keep).T
    for a in range(side):
        at = lead + tile_cols * a
        low = gk_t[keep + at + tile_cols - radius:keep + at + tile_cols, :]
        high = gk_t[at:at + radius + 1, :]
        gk_ref[a] = jnp.concatenate([low, high], axis=0).astype(bf16)

    for s in range(2):
        bytes_of(allq.at[s, 0], rsem.at[14 + s])
    for f in range(rows):
        at = slice(f * block, (f + 1) * block)
        gwi_ref[:, at] = allq[0, f % 2, f // 2].reshape(channels, block)
        gwo_ref[at, :] = allq[1, f % 2, f // 2].reshape(block, channels)

    bytes_of(x_send.at[pl.ds(0, n - 1)], ssem.at[0])
    bytes_of(g_send.at[pl.ds(0, n - 1)], ssem.at[1])
    bytes_of(gk_recv.at[pl.ds(0, n - 1)], ssem.at[2])
    bytes_of(o_send.at[pl.ds(0, n - 1)], ssem.at[3])
    for s in range(2):
        bytes_of(from_pair.at[s], ssem.at[4 + s])
        bytes_of(paired.at[s, pl.ds(0, pairs - 1)], ssem.at[6 + s])
        bytes_of(half.at[s, pl.ds(0, cols - 1)], ssem.at[8 + s])
        bytes_of(from_cols.at[s, pl.ds(0, cols - 1)], ssem.at[10 + s])
        bytes_of(allq.at[s, 0, pl.ds(0, pairs - 1)], ssem.at[12 + s])
        bytes_of(allq.at[s, 0], ssem.at[14 + s])


def hand_over_kernel(*refs):
    count = len(refs) // 2
    sem = refs[-1]
    copies = [
        pltpu.make_async_copy(refs[i], refs[count + i], sem.at[i]) for i in range(count)
    ]
    for copy in copies:
        copy.start()
    for copy in copies:
        copy.wait()


def fits(rows, cols, tile_rows, tile_cols, channels, hidden):
    n = rows * cols
    pixels = tile_rows * tile_cols
    radius = KS // 2
    return (
        channels % n == 0
        and channels // n == SUB
        and channels % LANE == 0
        and rows % 2 == 0
        and rows > 2
        and cols % 2 == 0
        and hidden == rows * channels
        and pixels == 2 * LANE
        and tile_cols == 2 * SUB
        and radius < min(tile_rows, tile_cols)
        and channels % (cols * 2 * SUB) == 0
    )


def fused_device(inputs, stored, upstream, weight_in, weight_out, kernel):
    rows, cols = lax.axis_size("row"), lax.axis_size("col")
    tile_rows, tile_cols, channels = stored.shape
    n, pixels, hidden = rows * cols, tile_rows * tile_cols, weight_in.shape[1]
    side = kernel.shape[0]
    radius = side // 2
    own = channels // n
    taps = pixels - tile_cols * radius - tile_cols + tile_cols * side
    width = round_up(taps + LANE - 1, LANE)
    keep = round_up(taps, LANE)
    span = 3 * pixels
    scale = 1.0 / math.sqrt(pixels * n)
    bf16, f32 = jnp.bfloat16, jnp.float32
    flat = (pixels, channels)
    piece = channels // cols
    pairs = rows // 2
    vmem = pl.BlockSpec(memory_space=pltpu.VMEM)
    results = pl.pallas_call(
        lambda *refs: fused_kernel(rows, cols, tile_cols, radius, scale, *refs),
        out_shape=(
            jax.ShapeDtypeStruct(flat, bf16),
            jax.ShapeDtypeStruct(weight_in.shape, bf16),
            jax.ShapeDtypeStruct(weight_out.shape, bf16),
            jax.ShapeDtypeStruct(kernel.shape, bf16),
        ),
        in_specs=[pl.BlockSpec(memory_space=pltpu.HBM)] * 6,
        out_specs=(vmem,) * 4,
        scratch_shapes=[pltpu.VMEM(flat, bf16)] * 3 + [
            pltpu.VMEM(weight_in.shape, bf16),
            pltpu.VMEM(weight_out.shape, bf16),
            pltpu.VMEM(kernel.shape, bf16),
        ] + [pltpu.VMEM((n, own, pixels), bf16)] * 6 + [
            pltpu.VMEM((2, 2, pairs, channels, channels), bf16),
            pltpu.VMEM((2, pairs, channels, channels), bf16),
            pltpu.VMEM((2, pairs, channels, channels), bf16),
            pltpu.VMEM((2, pairs, channels, channels), bf16),
            pltpu.VMEM((2, cols, piece, channels), bf16),
            pltpu.VMEM((2, cols, piece, channels), bf16),
            pltpu.VMEM((2, 2, pairs, cols, piece, channels), bf16),
            pltpu.VMEM((own, 2 * keep), bf16),
            pltpu.VMEM((n, own, 2 * keep), bf16),
            pltpu.VMEM((n, own, pixels), f32),
            pltpu.VMEM((own, n, pixels), f32),
            pltpu.VMEM((own, n, pixels), f32),
            pltpu.VMEM((own, n, pixels), f32),
            pltpu.VMEM((2, width, channels), f32),
            pltpu.VMEM((LANE, width), f32),
            pltpu.VMEM((2 * own, SUB, width), f32),
            pltpu.VMEM((2 * own, SUB, width), f32),
            pltpu.VMEM((2, LANE, pixels + span), f32),
            pltpu.VMEM((pixels, 3 * span), bf16),
            pltpu.VMEM((pixels, 3 * span), f32),
            pltpu.VMEM((n, 3 * span), bf16),
            pltpu.VMEM((2 * keep, channels), f32),
            pltpu.SemaphoreType.DMA((6,)),
            pltpu.SemaphoreType.DMA((16,)),
            pltpu.SemaphoreType.DMA((16,)),
        ],
        compiler_params=pltpu.CompilerParams(
            collective_id=0, has_side_effects=True, vmem_limit_bytes=64 * 1024 * 1024
        ),
    )(
        inputs.reshape(flat), stored.reshape(flat), upstream.reshape(flat),
        weight_in, weight_out, kernel,
    )
    results = pl.pallas_call(
        hand_over_kernel,
        out_shape=tuple(jax.ShapeDtypeStruct(r.shape, r.dtype) for r in results),
        in_specs=[pl.BlockSpec(memory_space=pl.ANY)] * len(results),
        out_specs=(pl.BlockSpec(memory_space=pl.ANY),) * len(results),
        scratch_shapes=[pltpu.SemaphoreType.DMA((len(results),))],
        compiler_params=pltpu.CompilerParams(vmem_limit_bytes=64 * 1024 * 1024),
    )(*results)
    return (results[0].reshape(stored.shape), *results[1:])


def per_device(inputs, stored, upstream, weight_in, weight_out, kernel):
    args = (inputs, stored, upstream, weight_in, weight_out, kernel)
    sizes = (lax.axis_size("row"), lax.axis_size("col"))
    if fits(*sizes, *stored.shape, weight_in.shape[1]):
        return fused_device(*args)
    return sweep_device(*args)


def solution(mesh):
    return jax.shard_map(
        per_device,
        mesh=mesh,
        in_specs=(
            P("row", "col", None),
            P("row", "col", None),
            P("row", "col", None),
            P(),
            P(),
            P(),
        ),
        out_specs=(P("row", "col", None), P(), P(), P()),
        check_vma=False,
    )
```

```python
import math

import jax
import jax.numpy as jnp
from jax import lax
from jax.experimental import pallas as pl
from jax.experimental.pallas import tpu as pltpu
from jax.sharding import PartitionSpec as P

KS = 27


gelu_coef = 0.044715
root_coef = math.sqrt(2.0 / math.pi)


def padded_2(block, sides, width):
    for axis, dim in sides:
        count = lax.axis_size(axis)
        forward = [(i, i + 1) for i in range(count - 1)]
        backward = [(target, source) for source, target in forward]
        low = lax.ppermute(
            lax.slice_in_dim(block, block.shape[dim] - width, None, axis=dim), axis, forward
        )
        high = lax.ppermute(lax.slice_in_dim(block, 0, width, axis=dim), axis, backward)
        block = jnp.concatenate([low, block, high], axis=dim)
    return block


def gelu_parts(values):
    tanh_part = jnp.tanh(root_coef * (values + gelu_coef * values * values * values))
    result = 0.5 * values * (1.0 + tanh_part)
    slopes = 0.5 * (1.0 + tanh_part) + 0.5 * values * (1.0 - tanh_part * tanh_part) * root_coef * (
        1.0 + 3.0 * gelu_coef * values * values
    )
    return (result, slopes)


def sweep_device(inputs, stored, upstream, weight_in, weight_out, kernel):
    tile_rows, tile_cols, channels = stored.shape
    radius = KS // 2
    flat_z = stored.reshape(tile_rows * tile_cols, channels)
    flat_g = upstream.reshape(tile_rows * tile_cols, channels)
    hidden = jnp.dot(flat_z, weight_in, preferred_element_type=jnp.float32)
    values, slopes = gelu_parts(hidden)
    active = values.astype(jnp.bfloat16)
    back_proj = jnp.einsum("nc,fc->nf", flat_g, weight_out, preferred_element_type=jnp.float32)
    grad_hidden = (back_proj * slopes).astype(jnp.bfloat16)
    grad_flat = (
        flat_g.astype(jnp.float32)
        + jnp.einsum("nf,cf->nc", grad_hidden, weight_in, preferred_element_type=jnp.float32)
    ).astype(jnp.bfloat16)
    sum_in = jnp.einsum("nc,nf->cf", flat_z, grad_hidden, preferred_element_type=jnp.float32)
    sum_out = jnp.einsum("nf,nc->fc", active, flat_g, preferred_element_type=jnp.float32)
    grad_mid = grad_flat.reshape(tile_rows, tile_cols, channels)
    padded = padded_2(grad_mid, (("row", 0), ("col", 1)), radius)
    kernel_wide = kernel.astype(jnp.float32)

    def sweep(row_off, state_pair):
        accumulated, kernel_sums = state_pair
        slab_rows = lax.dynamic_slice_in_dim(padded, 2 * radius - row_off, tile_rows, 0)
        tap_row = lax.dynamic_index_in_dim(kernel_wide, row_off, 0, keepdims=False)
        tap_sums = []
        for offset in range(KS):
            shifted = slab_rows[:, 2 * radius - offset : 2 * radius - offset + tile_cols].astype(
                jnp.float32
            )
            accumulated = accumulated + tap_row[offset] * shifted
            tap_sums.append(jnp.sum(inputs.astype(jnp.float32) * shifted, axis=(0, 1)))
        kernel_sums = lax.dynamic_update_index_in_dim(kernel_sums, jnp.stack(tap_sums), row_off, 0)
        return (accumulated, kernel_sums)

    start = (
        jnp.zeros((tile_rows, tile_cols, channels), jnp.float32),
        jnp.zeros((KS, KS, channels), jnp.float32),
    )
    accumulated, kernel_sums = lax.fori_loop(0, KS, sweep, start)
    grad_inputs = (grad_mid.astype(jnp.float32) + accumulated).astype(jnp.bfloat16)
    devices_all = lax.axis_size("row") * lax.axis_size("col")
    pixel_count = tile_rows * tile_cols * devices_all
    grad_scale = 1.0 / math.sqrt(pixel_count)
    total_in, total_out, total_kernel = lax.psum((sum_in, sum_out, kernel_sums), ("row", "col"))
    final_in = (total_in * grad_scale).astype(jnp.bfloat16)
    final_out = (total_out * grad_scale).astype(jnp.bfloat16)
    final_kernel = (total_kernel * grad_scale).astype(jnp.bfloat16)
    return (grad_inputs, final_in, final_out, final_kernel)


MESH = pl.DeviceIdType.MESH
LANE = 128
SUB = 8


def round_up(value, unit):
    return -(-value // unit) * unit


def dot(a, b, over_a, over_b):
    return lax.dot_general(
        a, b, (((over_a,), (over_b,)), ((), ())), preferred_element_type=jnp.float32
    )


def roll_left(v, shift, axis):
    size = v.shape[axis]
    shift = shift % size
    return v if shift == 0 else pltpu.roll(v, size - shift, axis)


def down(v, count):
    if count == 0:
        return v
    blank = jnp.zeros((abs(count), v.shape[1]), v.dtype)
    if count > 0:
        return jnp.concatenate([blank, v[:-count]], axis=0)
    return jnp.concatenate([v[-count:], blank], axis=0)


def bytes_of(ref, sem):
    pltpu.make_async_copy(ref, ref, sem).wait()


def fused_kernel(
    rows, cols, tile_cols, radius, scale,
    x_hbm, z_hbm, g_hbm, wi_hbm, wo_hbm, k_hbm,
    gi_ref, gwi_ref, gwo_ref, gk_ref,
    x_ref, z_ref, g_ref, wi_ref, wo_ref, k_ref,
    x_send, x_recv, g_send, g_recv, o_send, o_recv,
    part, from_pair, paired, from_rows, half, from_cols, allq, gk_send, gk_recv,
    wide, x3, g3, o3, taps, taps_t, skew, folded, bands, k_mat, m_mat, x_sh, gk_t, inner,
    isem, ssem, rsem,
):
    n = rows * cols
    pixels, channels = z_ref.shape
    own = channels // n
    side = k_ref.shape[0]
    lead = pixels - tile_cols * radius - tile_cols
    width = skew.shape[2]
    span = 3 * pixels
    per_block = LANE // tile_cols
    chunks = pixels // tile_cols
    my_row, my_col = lax.axis_index("row"), lax.axis_index("col")
    me = my_row * cols + my_col
    pairs = rows // 2
    my_pair, core = my_row // 2, lax.rem(my_row, 2)
    other = 1 - core
    f32, bf16 = jnp.float32, jnp.bfloat16

    def send(src, dst, phase, row, col):
        pltpu.make_async_remote_copy(
            src_ref=src, dst_ref=dst, send_sem=ssem.at[phase], recv_sem=rsem.at[phase],
            device_id=(row, col), device_id_type=MESH,
        ).start()

    def sum_pair(s):
        bytes_of(from_pair.at[s], rsem.at[4 + s])
        for p in range(pairs):
            paired[s, p] = (
                part[s, core, p].astype(f32) + from_pair[s, p].astype(f32)).astype(bf16)
        for p in range(1, pairs):
            to = lax.rem(my_pair + p, pairs)
            send(paired.at[s, to], from_rows.at[s, my_pair], 6 + s, 2 * to + core, my_col)
        from_rows[s, pl.ds(my_pair, 1)] = paired[s, pl.ds(my_pair, 1)]

    def sum_rows(s):
        bytes_of(from_rows.at[s, pl.ds(0, pairs - 1)], rsem.at[6 + s])
        v = from_rows[s, 0].astype(f32)
        for p in range(1, pairs):
            v = v + from_rows[s, p].astype(f32)
        half[s] = v.reshape(half.shape[1:]).astype(bf16)
        for p in range(1, cols):
            c = lax.rem(my_col + p, cols)
            send(half.at[s, c], from_cols.at[s, my_col], 8 + s, my_row, c)
        from_cols[s, pl.ds(my_col, 1)] = half[s, pl.ds(my_col, 1)]

    def sum_cols(s):
        bytes_of(from_cols.at[s, pl.ds(0, cols - 1)], rsem.at[8 + s])
        v = from_cols[s, 0].astype(f32)
        for c in range(1, cols):
            v = v + from_cols[s, c].astype(f32)
        mine = allq.at[s, core, my_pair, my_col]
        mine[...] = (v * scale).astype(bf16)
        for p in range(1, cols):
            send(mine, mine, 10 + s, my_row, lax.rem(my_col + p, cols))

    def share_rows(s):
        bytes_of(allq.at[s, 0, 0, pl.ds(0, cols - 1)], rsem.at[10 + s])
        mine = allq.at[s, core, my_pair]
        for p in range(1, pairs):
            to = lax.rem(my_pair + p, pairs)
            send(mine, mine, 12 + s, 2 * to + core, my_col)

    def share_pair(s):
        bytes_of(allq.at[s, 0, pl.ds(0, pairs - 1)], rsem.at[12 + s])
        mine = allq.at[s, core]
        send(mine, mine, 14 + s, my_row + other - core, my_col)

    row_at = [lax.rem(my_row + r, rows) for r in range(rows)]
    col_at = [lax.rem(my_col + c, cols) for c in range(cols)]

    def to_all(fn):
        for r in range(rows):
            for c in range(cols):
                if r + c:
                    fn(row_at[r] * cols + col_at[c], row_at[r], col_at[c])

    loads = [
        pltpu.make_async_copy(source, target, isem.at[i])
        for i, (source, target) in enumerate((
            (x_hbm, x_ref), (z_hbm, z_ref), (g_hbm, g_ref),
            (wi_hbm, wi_ref), (wo_hbm, wo_ref), (k_hbm, k_ref),
        ))
    ]
    for load in loads:
        load.start()
    barrier = pltpu.get_barrier_semaphore()
    to_all(lambda t, r, c: pl.semaphore_signal(
        barrier, inc=1, device_id=(r, c), device_id_type=MESH))

    for load in loads:
        load.wait()
    z, g = z_ref[...], g_ref[...]
    total = g.astype(f32)
    block = wi_ref.shape[1] // rows
    for f in range(rows):
        w_in = wi_ref[:, f * block:(f + 1) * block]
        w_out = wo_ref[f * block:(f + 1) * block, :]
        values, slopes = gelu_parts(dot(z, w_in, 1, 0))
        active = values.astype(bf16)
        grad_hidden = (dot(g, w_out, 1, 1) * slopes).astype(bf16)
        total = total + dot(grad_hidden, w_in, 1, 1)
        part[0, f % 2, f // 2] = dot(z, grad_hidden, 0, 0).astype(bf16)
        part[1, f % 2, f // 2] = dot(active, g, 0, 0).astype(bf16)
        if f == 0:
            x_send[...] = x_ref[...].astype(f32).T.reshape(n, own, pixels).astype(bf16)
            x_recv[pl.ds(me, 1)] = x_send[pl.ds(me, 1)]
            pl.semaphore_wait(barrier, n - 1)
            to_all(lambda t, r, c: send(x_send.at[t], x_recv.at[me], 0, r, c))
    g_send[...] = total.T.reshape(n, own, pixels).astype(bf16)
    g_recv[pl.ds(me, 1)] = g_send[pl.ds(me, 1)]
    to_all(lambda t, r, c: send(g_send.at[t], g_recv.at[me], 1, r, c))
    for s in range(2):
        send(part.at[s, other], from_pair.at[s], 4 + s, my_row + other - core, my_col)

    taps[...] = jnp.zeros_like(taps)
    for a in range(side):
        tap = k_ref[a].astype(f32)
        at = lead + tile_cols * a
        taps[0, at:at + radius + 1, :] = tap[radius:]
        taps[1, at + tile_cols - radius:at + tile_cols, :] = tap[:radius]
    lanes_at = pl.multiple_of(me * own // LANE * LANE, LANE)
    for sign in range(2):
        taps_t[...] = taps[sign, :, pl.ds(lanes_at, LANE)].T
        line = taps_t[pl.ds(pl.multiple_of(lax.rem(me * own, LANE), SUB), own), :]
        for t in range(SUB):
            skew[sign * own:(sign + 1) * own, t, :] = pltpu.roll(line, t, 1) if t else line

    at_or_after = (
        lax.broadcasted_iota(jnp.int32, (tile_cols, span), 1) % tile_cols
        >= lax.broadcasted_iota(jnp.int32, (tile_cols, span), 0)
    )
    offsets = (-1, 0, 1)
    tile = lax.broadcasted_iota(jnp.int32, (n, pixels), 0) % cols
    inner[0] = jnp.where(tile > 0, 1.0, 0.0)
    inner[1] = jnp.where(tile < cols - 1, 1.0, 0.0)

    def aside(v, d_col):
        if d_col == 0:
            return v
        return roll_left(v, d_col, 0) * inner[0 if d_col < 0 else 1]


    sum_pair(0)
    sum_pair(1)
    bytes_of(x_recv.at[pl.ds(0, n - 1)], rsem.at[0])
    wide[...] = x_recv[...].astype(f32)
    for c in range(own):
        x3[c] = wide[:, c, :]
    bytes_of(g_recv.at[pl.ds(0, n - 1)], rsem.at[1])
    wide[...] = g_recv[...].astype(f32)
    for c in range(own):
        g3[c] = wide[:, c, :]

    def correlate(c):
        here = x3[c]
        for i, d_col in enumerate(offsets):
            beside = aside(here, d_col)
            for j, d_row in enumerate(offsets):
                at = i * span + j * pixels
                x_sh[:, at:at + pixels] = down(beside, -d_row * cols).astype(bf16)
        m_mat[...] = dot(g3[c].astype(bf16), x_sh[...], 0, 0)

        def piece(q, i):
            return m_mat[q * tile_cols:(q + 1) * tile_cols, i * span:(i + 1) * span]

        def lagged(q, sign):
            after, before = ((1, 2), (0, 1))[sign]
            out = jnp.zeros((tile_cols, span), f32)
            if q >= 1:
                out = jnp.where(at_or_after, piece(q - 1, after), 0.0)
            if q < chunks:
                out = out + jnp.where(at_or_after, 0.0, piece(q, before))
            return out

        for sign in range(2):
            parts = []
            for i in range(per_block):
                v = jnp.zeros((tile_cols, width), f32)
                for q in range(i, chunks + 1, per_block):
                    skip = q // per_block * LANE
                    piece_q = lagged(q, sign)[:, skip:skip + width]
                    missing = width - piece_q.shape[1]
                    if missing:
                        piece_q = jnp.concatenate(
                            [piece_q, jnp.zeros((tile_cols, missing), f32)], axis=1)
                    v = v + piece_q
                parts.append(v)
            while len(parts) > 1:
                m = len(parts) // 2
                parts = [parts[i] + roll_left(parts[i + m], m * tile_cols, 1) for i in range(m)]
            v = parts[0]
            m = tile_cols // 2
            while m >= SUB:
                v = v[:m] + roll_left(v[m:], m, 1)
                m //= 2
            folded[sign * own + c] = v

    pl.loop(0, own // 2)(correlate)
    sum_rows(0)
    sum_rows(1)
    pl.loop(own // 2, own)(correlate)

    lines = folded[:, 0, :]
    for t in range(1, SUB):
        lines = lines + roll_left(folded[:, t, :], t, 1)
    keep = gk_send.shape[1] // 2
    lines = (lines * scale)[:, :keep]
    gk_send[...] = jnp.concatenate([lines[:own], lines[own:]], axis=1).astype(bf16)
    spot = gk_recv.at[core, my_pair, my_col]
    spot[...] = gk_send[...]
    for p in range(1, cols):
        send(gk_send, spot, 2, my_row, col_at[p])

    sum_cols(0)
    sum_cols(1)

    bands[...] = jnp.zeros_like(bands)

    def convolve(c):
        for sign in range(2):
            v = skew[sign * own + c]
            m = SUB
            while m < tile_cols:
                v = jnp.concatenate([v, pltpu.roll(v, m, 1)], axis=0)
                m *= 2
            parts = [v]
            while len(parts) < per_block:
                m = len(parts) * tile_cols
                parts = parts + [pltpu.roll(u, m, 1) for u in parts]
            for i, u in enumerate(parts):
                bands[sign, i * tile_cols:(i + 1) * tile_cols, pixels:pixels + width] = u

        def band(q, sign):
            at = q % per_block * tile_cols
            skip = pixels - q // per_block * LANE
            return bands[sign, at:at + tile_cols, skip:skip + span]

        for q in range(chunks):
            at = slice(q * tile_cols, (q + 1) * tile_cols)
            k_mat[at, :span] = jnp.where(at_or_after, band(q + 1, 1), 0.0).astype(bf16)
            k_mat[at, span:2 * span] = jnp.where(
                at_or_after, band(q + 1, 0), band(q, 1)).astype(bf16)
            k_mat[at, 2 * span:] = jnp.where(at_or_after, 0.0, band(q, 0)).astype(bf16)
        here = g3[c]
        spread = dot(here.astype(bf16), k_mat[...], 1, 0)
        result = here
        for i, d_col in enumerate(offsets):
            at = i * span
            beside = spread[:, at + pixels:at + 2 * pixels]
            beside = beside + down(spread[:, at:at + pixels], -cols)
            beside = beside + down(spread[:, at + 2 * pixels:at + span], cols)
            result = result + aside(beside, -d_col)
        o3[c] = result

    pl.loop(0, own // 2)(convolve)
    share_rows(0)
    share_rows(1)
    bytes_of(gk_recv.at[0, 0, pl.ds(0, cols - 1)], rsem.at[2])
    spots = gk_recv.at[core, my_pair]
    for p in range(1, pairs):
        send(spots, spots, 16, 2 * lax.rem(my_pair + p, pairs) + core, my_col)
    pl.loop(own // 2, own)(convolve)

    for c in range(own):
        wide[:, c, :] = o3[c]
    o_send[...] = wide[...].astype(bf16)
    o_recv[pl.ds(me, 1)] = o_send[pl.ds(me, 1)]
    to_all(lambda t, r, c: send(o_send.at[t], o_recv.at[me], 3, r, c))

    share_pair(0)
    share_pair(1)
    bytes_of(gk_recv.at[0, pl.ds(0, pairs - 1)], rsem.at[16])
    send(gk_recv.at[core], gk_recv.at[core], 17, my_row + other - core, my_col)

    bytes_of(o_recv.at[pl.ds(0, n - 1)], rsem.at[3])
    gi_ref[...] = o_recv[...].astype(f32).reshape(channels, pixels).T.astype(bf16)

    bytes_of(gk_recv.at[0], rsem.at[17])
    share = cols * own
    for r in range(rows):
        gk_t[:, r * share:(r + 1) * share] = (
            gk_recv[r % 2, r // 2].astype(f32).reshape(share, 2 * keep).T)
    for a in range(side):
        at = lead + tile_cols * a
        low = gk_t[keep + at + tile_cols - radius:keep + at + tile_cols, :]
        high = gk_t[at:at + radius + 1, :]
        gk_ref[a] = jnp.concatenate([low, high], axis=0).astype(bf16)

    for s in range(2):
        bytes_of(allq.at[s, 0], rsem.at[14 + s])
    for f in range(rows):
        at = slice(f * block, (f + 1) * block)
        gwi_ref[:, at] = allq[0, f % 2, f // 2].reshape(channels, block)
        gwo_ref[at, :] = allq[1, f % 2, f // 2].reshape(block, channels)

    bytes_of(x_send.at[pl.ds(0, n - 1)], ssem.at[0])
    bytes_of(g_send.at[pl.ds(0, n - 1)], ssem.at[1])
    bytes_of(gk_recv.at[0, 0, pl.ds(0, cols - 1)], ssem.at[2])
    bytes_of(gk_recv.at[0, pl.ds(0, pairs - 1)], ssem.at[16])
    bytes_of(gk_recv.at[0], ssem.at[17])
    bytes_of(o_send.at[pl.ds(0, n - 1)], ssem.at[3])
    for s in range(2):
        bytes_of(from_pair.at[s], ssem.at[4 + s])
        bytes_of(paired.at[s, pl.ds(0, pairs - 1)], ssem.at[6 + s])
        bytes_of(half.at[s, pl.ds(0, cols - 1)], ssem.at[8 + s])
        bytes_of(from_cols.at[s, pl.ds(0, cols - 1)], ssem.at[10 + s])
        bytes_of(allq.at[s, 0, pl.ds(0, pairs - 1)], ssem.at[12 + s])
        bytes_of(allq.at[s, 0], ssem.at[14 + s])


def hand_over_kernel(count, *refs):
    ins, outs, held, sems = refs[:count], refs[count:2 * count], refs[2 * count:-1], refs[-1]
    first = [pltpu.make_async_copy(ins[i], held[i], sems.at[0, i]) for i in range(count)]
    then = [pltpu.make_async_copy(held[i], outs[i], sems.at[1, i]) for i in range(count)]
    for copy in first:
        copy.start()
    for i in range(count):
        first[i].wait()
        then[i].start()
    for copy in then:
        copy.wait()


def fits(rows, cols, tile_rows, tile_cols, channels, hidden):
    n = rows * cols
    pixels = tile_rows * tile_cols
    radius = KS // 2
    return (
        channels % n == 0
        and channels // n == SUB
        and channels % LANE == 0
        and rows % 2 == 0
        and rows > 2
        and cols % 2 == 0
        and hidden == rows * channels
        and pixels == 2 * LANE
        and tile_cols == 2 * SUB
        and radius < min(tile_rows, tile_cols)
        and channels % (cols * 2 * SUB) == 0
    )


def fused_device(inputs, stored, upstream, weight_in, weight_out, kernel):
    rows, cols = lax.axis_size("row"), lax.axis_size("col")
    tile_rows, tile_cols, channels = stored.shape
    n, pixels, hidden = rows * cols, tile_rows * tile_cols, weight_in.shape[1]
    side = kernel.shape[0]
    radius = side // 2
    own = channels // n
    taps = pixels - tile_cols * radius - tile_cols + tile_cols * side
    width = round_up(taps + LANE - 1, LANE)
    keep = round_up(taps, LANE)
    span = 3 * pixels
    scale = 1.0 / math.sqrt(pixels * n)
    bf16, f32 = jnp.bfloat16, jnp.float32
    flat = (pixels, channels)
    piece = channels // cols
    pairs = rows // 2
    vmem = pl.BlockSpec(memory_space=pltpu.VMEM)
    results = pl.pallas_call(
        lambda *refs: fused_kernel(rows, cols, tile_cols, radius, scale, *refs),
        out_shape=(
            jax.ShapeDtypeStruct(flat, bf16),
            jax.ShapeDtypeStruct(weight_in.shape, bf16),
            jax.ShapeDtypeStruct(weight_out.shape, bf16),
            jax.ShapeDtypeStruct(kernel.shape, bf16),
        ),
        in_specs=[pl.BlockSpec(memory_space=pltpu.HBM)] * 6,
        out_specs=(vmem,) * 4,
        scratch_shapes=[pltpu.VMEM(flat, bf16)] * 3 + [
            pltpu.VMEM(weight_in.shape, bf16),
            pltpu.VMEM(weight_out.shape, bf16),
            pltpu.VMEM(kernel.shape, bf16),
        ] + [pltpu.VMEM((n, own, pixels), bf16)] * 6 + [
            pltpu.VMEM((2, 2, pairs, channels, channels), bf16),
            pltpu.VMEM((2, pairs, channels, channels), bf16),
            pltpu.VMEM((2, pairs, channels, channels), bf16),
            pltpu.VMEM((2, pairs, channels, channels), bf16),
            pltpu.VMEM((2, cols, piece, channels), bf16),
            pltpu.VMEM((2, cols, piece, channels), bf16),
            pltpu.VMEM((2, 2, pairs, cols, piece, channels), bf16),
            pltpu.VMEM((own, 2 * keep), bf16),
            pltpu.VMEM((2, pairs, cols, own, 2 * keep), bf16),
            pltpu.VMEM((n, own, pixels), f32),
            pltpu.VMEM((own, n, pixels), f32),
            pltpu.VMEM((own, n, pixels), f32),
            pltpu.VMEM((own, n, pixels), f32),
            pltpu.VMEM((2, width, channels), f32),
            pltpu.VMEM((LANE, width), f32),
            pltpu.VMEM((2 * own, SUB, width), f32),
            pltpu.VMEM((2 * own, SUB, width), f32),
            pltpu.VMEM((2, LANE, pixels + span), f32),
            pltpu.VMEM((pixels, 3 * span), bf16),
            pltpu.VMEM((pixels, 3 * span), f32),
            pltpu.VMEM((n, 3 * span), bf16),
            pltpu.VMEM((2 * keep, channels), f32),
            pltpu.VMEM((2, n, pixels), f32),
            pltpu.SemaphoreType.DMA((6,)),
            pltpu.SemaphoreType.DMA((18,)),
            pltpu.SemaphoreType.DMA((18,)),
        ],
        compiler_params=pltpu.CompilerParams(
            collective_id=0, has_side_effects=True, vmem_limit_bytes=64 * 1024 * 1024
        ),
    )(
        inputs.reshape(flat), stored.reshape(flat), upstream.reshape(flat),
        weight_in, weight_out, kernel,
    )
    results = pl.pallas_call(
        lambda *refs: hand_over_kernel(len(results), *refs),
        out_shape=tuple(jax.ShapeDtypeStruct(r.shape, r.dtype) for r in results),
        in_specs=[pl.BlockSpec(memory_space=pl.ANY)] * len(results),
        out_specs=(pl.BlockSpec(memory_space=pl.ANY),) * len(results),
        scratch_shapes=[pltpu.VMEM(r.shape, r.dtype) for r in results]
        + [pltpu.SemaphoreType.DMA((2, len(results)))],
        compiler_params=pltpu.CompilerParams(vmem_limit_bytes=64 * 1024 * 1024),
    )(*results)
    return (results[0].reshape(stored.shape), *results[1:])


def per_device(inputs, stored, upstream, weight_in, weight_out, kernel):
    args = (inputs, stored, upstream, weight_in, weight_out, kernel)
    sizes = (lax.axis_size("row"), lax.axis_size("col"))
    if fits(*sizes, *stored.shape, weight_in.shape[1]):
        return fused_device(*args)
    return sweep_device(*args)


def solution(mesh):
    return jax.shard_map(
        per_device,
        mesh=mesh,
        in_specs=(
            P("row", "col", None),
            P("row", "col", None),
            P("row", "col", None),
            P(),
            P(),
            P(),
        ),
        out_specs=(P("row", "col", None), P(), P(), P()),
        check_vma=False,
    )
```

```python
import math

import jax
import jax.numpy as jnp
from jax import lax
from jax.experimental import pallas as pl
from jax.experimental.pallas import tpu as pltpu
from jax.sharding import PartitionSpec as P

KS = 27


gelu_coef = 0.044715
root_coef = math.sqrt(2.0 / math.pi)


def padded_2(block, sides, width):
    for axis, dim in sides:
        count = lax.axis_size(axis)
        forward = [(i, i + 1) for i in range(count - 1)]
        backward = [(target, source) for source, target in forward]
        low = lax.ppermute(
            lax.slice_in_dim(block, block.shape[dim] - width, None, axis=dim), axis, forward
        )
        high = lax.ppermute(lax.slice_in_dim(block, 0, width, axis=dim), axis, backward)
        block = jnp.concatenate([low, block, high], axis=dim)
    return block


def gelu_parts(values):
    tanh_part = jnp.tanh(root_coef * (values + gelu_coef * values * values * values))
    result = 0.5 * values * (1.0 + tanh_part)
    slopes = 0.5 * (1.0 + tanh_part) + 0.5 * values * (1.0 - tanh_part * tanh_part) * root_coef * (
        1.0 + 3.0 * gelu_coef * values * values
    )
    return (result, slopes)


def sweep_device(inputs, stored, upstream, weight_in, weight_out, kernel):
    tile_rows, tile_cols, channels = stored.shape
    radius = KS // 2
    flat_z = stored.reshape(tile_rows * tile_cols, channels)
    flat_g = upstream.reshape(tile_rows * tile_cols, channels)
    hidden = jnp.dot(flat_z, weight_in, preferred_element_type=jnp.float32)
    values, slopes = gelu_parts(hidden)
    active = values.astype(jnp.bfloat16)
    back_proj = jnp.einsum("nc,fc->nf", flat_g, weight_out, preferred_element_type=jnp.float32)
    grad_hidden = (back_proj * slopes).astype(jnp.bfloat16)
    grad_flat = (
        flat_g.astype(jnp.float32)
        + jnp.einsum("nf,cf->nc", grad_hidden, weight_in, preferred_element_type=jnp.float32)
    ).astype(jnp.bfloat16)
    sum_in = jnp.einsum("nc,nf->cf", flat_z, grad_hidden, preferred_element_type=jnp.float32)
    sum_out = jnp.einsum("nf,nc->fc", active, flat_g, preferred_element_type=jnp.float32)
    grad_mid = grad_flat.reshape(tile_rows, tile_cols, channels)
    padded = padded_2(grad_mid, (("row", 0), ("col", 1)), radius)
    kernel_wide = kernel.astype(jnp.float32)

    def sweep(row_off, state_pair):
        accumulated, kernel_sums = state_pair
        slab_rows = lax.dynamic_slice_in_dim(padded, 2 * radius - row_off, tile_rows, 0)
        tap_row = lax.dynamic_index_in_dim(kernel_wide, row_off, 0, keepdims=False)
        tap_sums = []
        for offset in range(KS):
            shifted = slab_rows[:, 2 * radius - offset : 2 * radius - offset + tile_cols].astype(
                jnp.float32
            )
            accumulated = accumulated + tap_row[offset] * shifted
            tap_sums.append(jnp.sum(inputs.astype(jnp.float32) * shifted, axis=(0, 1)))
        kernel_sums = lax.dynamic_update_index_in_dim(kernel_sums, jnp.stack(tap_sums), row_off, 0)
        return (accumulated, kernel_sums)

    start = (
        jnp.zeros((tile_rows, tile_cols, channels), jnp.float32),
        jnp.zeros((KS, KS, channels), jnp.float32),
    )
    accumulated, kernel_sums = lax.fori_loop(0, KS, sweep, start)
    grad_inputs = (grad_mid.astype(jnp.float32) + accumulated).astype(jnp.bfloat16)
    devices_all = lax.axis_size("row") * lax.axis_size("col")
    pixel_count = tile_rows * tile_cols * devices_all
    grad_scale = 1.0 / math.sqrt(pixel_count)
    total_in, total_out, total_kernel = lax.psum((sum_in, sum_out, kernel_sums), ("row", "col"))
    final_in = (total_in * grad_scale).astype(jnp.bfloat16)
    final_out = (total_out * grad_scale).astype(jnp.bfloat16)
    final_kernel = (total_kernel * grad_scale).astype(jnp.bfloat16)
    return (grad_inputs, final_in, final_out, final_kernel)


MESH = pl.DeviceIdType.MESH
LANE = 128
SUB = 8


def round_up(value, unit):
    return -(-value // unit) * unit


def dot(a, b, over_a, over_b):
    return lax.dot_general(
        a, b, (((over_a,), (over_b,)), ((), ())), preferred_element_type=jnp.float32
    )


def roll_left(v, shift, axis):
    size = v.shape[axis]
    shift = shift % size
    return v if shift == 0 else pltpu.roll(v, size - shift, axis)


def down(v, count):
    if count == 0:
        return v
    blank = jnp.zeros((abs(count), v.shape[1]), v.dtype)
    if count > 0:
        return jnp.concatenate([blank, v[:-count]], axis=0)
    return jnp.concatenate([v[-count:], blank], axis=0)


def bytes_of(ref, sem):
    pltpu.make_async_copy(ref, ref, sem).wait()


def fused_kernel(
    rows, cols, tile_cols, radius, scale,
    x_hbm, z_hbm, g_hbm, wi_hbm, wo_hbm, k_hbm,
    gi_ref, gwi_ref, gwo_ref, gk_ref,
    x_ref, z_ref, g_ref, wi_ref, wo_ref, k_ref,
    x_send, x_recv, g_send, g_recv, o_send, o_recv,
    part, from_pair, paired, from_rows, half, from_cols, allq,
    paired_b, from_cols_b, half_b, from_rows_b, all_b, gk_send, gk_recv,
    wide, x3, g3, o3, taps, taps_t, skew, folded, bands, k_mat, m_mat, x_sh, gk_t, inner,
    isem, ssem, rsem,
):
    n = rows * cols
    pixels, channels = z_ref.shape
    own = channels // n
    side = k_ref.shape[0]
    lead = pixels - tile_cols * radius - tile_cols
    width = skew.shape[2]
    span = 3 * pixels
    per_block = LANE // tile_cols
    chunks = pixels // tile_cols
    my_row, my_col = lax.axis_index("row"), lax.axis_index("col")
    me = my_row * cols + my_col
    pairs = rows // 2
    piece = channels // cols
    my_pair, core = my_row // 2, lax.rem(my_row, 2)
    other = 1 - core
    f32, bf16 = jnp.float32, jnp.bfloat16

    def send(src, dst, phase, row, col):
        pltpu.make_async_remote_copy(
            src_ref=src, dst_ref=dst, send_sem=ssem.at[phase], recv_sem=rsem.at[phase],
            device_id=(row, col), device_id_type=MESH,
        ).start()

    def to_pairs(fn):
        for p in range(1, pairs):
            to = lax.rem(my_pair + p, pairs)
            fn(to, 2 * to + core, my_col)

    def to_cols(fn):
        for p in range(1, cols):
            fn(col_at[p], my_row, col_at[p])

    def added(ref):
        v = ref[0].astype(f32)
        for i in range(1, ref.shape[0]):
            v = v + ref[i].astype(f32)
        return v

    def sum_pair():
        bytes_of(from_pair.at[0], rsem.at[4])
        for p in range(pairs):
            paired[0, p] = (
                part[0, core, p].astype(f32) + from_pair[0, p].astype(f32)).astype(bf16)
        to_pairs(lambda t, r, c: send(paired.at[0, t], from_rows.at[my_pair], 6, r, c))
        from_rows[pl.ds(my_pair, 1)] = paired[0, pl.ds(my_pair, 1)]
        bytes_of(from_pair.at[1], rsem.at[5])
        for p in range(pairs):
            v = (part[1, core, p].astype(f32) + from_pair[1, p].astype(f32)).astype(bf16)
            for c in range(cols):
                paired_b[c, p] = v[c * piece:(c + 1) * piece]
        to_cols(lambda t, r, c: send(paired_b.at[t], from_cols_b.at[my_col], 7, r, c))
        from_cols_b[pl.ds(my_col, 1)] = paired_b[pl.ds(my_col, 1)]

    def sum_next():
        bytes_of(from_rows.at[pl.ds(0, pairs - 1)], rsem.at[6])
        half[...] = added(from_rows).reshape(half.shape).astype(bf16)
        to_cols(lambda t, r, c: send(half.at[t], from_cols.at[my_col], 8, r, c))
        from_cols[pl.ds(my_col, 1)] = half[pl.ds(my_col, 1)]
        bytes_of(from_cols_b.at[pl.ds(0, cols - 1)], rsem.at[7])
        half_b[...] = added(from_cols_b).astype(bf16)
        to_pairs(lambda t, r, c: send(half_b.at[t], from_rows_b.at[my_pair], 9, r, c))
        from_rows_b[pl.ds(my_pair, 1)] = half_b[pl.ds(my_pair, 1)]

    def sum_last():
        bytes_of(from_rows_b.at[pl.ds(0, pairs - 1)], rsem.at[9])
        mine_b = all_b.at[core, my_col, my_pair]
        mine_b[...] = (added(from_rows_b) * scale).astype(bf16)
        to_pairs(lambda t, r, c: send(mine_b, mine_b, 11, r, c))
        bytes_of(from_cols.at[pl.ds(0, cols - 1)], rsem.at[8])
        mine = allq.at[core, my_pair, my_col]
        mine[...] = (added(from_cols) * scale).astype(bf16)
        to_cols(lambda t, r, c: send(mine, mine, 10, r, c))

    def share_first():
        bytes_of(all_b.at[0, 0, pl.ds(0, pairs - 1)], rsem.at[11])
        mine_b = all_b.at[core, my_col]
        to_cols(lambda t, r, c: send(mine_b, mine_b, 13, r, c))

    def share_next():
        bytes_of(allq.at[0, 0, pl.ds(0, cols - 1)], rsem.at[10])
        mine = allq.at[core, my_pair]
        to_pairs(lambda t, r, c: send(mine, mine, 12, r, c))

    def share_pair():
        bytes_of(all_b.at[0, pl.ds(0, cols - 1)], rsem.at[13])
        send(all_b.at[core], all_b.at[core], 15, my_row + other - core, my_col)
        bytes_of(allq.at[0, pl.ds(0, pairs - 1)], rsem.at[12])
        send(allq.at[core], allq.at[core], 14, my_row + other - core, my_col)

    row_at = [lax.rem(my_row + r, rows) for r in range(rows)]
    col_at = [lax.rem(my_col + c, cols) for c in range(cols)]

    def to_all(fn):
        for r in range(rows):
            for c in range(cols):
                if r + c:
                    fn(row_at[r] * cols + col_at[c], row_at[r], col_at[c])

    loads = [
        pltpu.make_async_copy(source, target, isem.at[i])
        for i, (source, target) in enumerate((
            (x_hbm, x_ref), (z_hbm, z_ref), (g_hbm, g_ref),
            (wi_hbm, wi_ref), (wo_hbm, wo_ref), (k_hbm, k_ref),
        ))
    ]
    for load in loads:
        load.start()
    barrier = pltpu.get_barrier_semaphore()
    to_all(lambda t, r, c: pl.semaphore_signal(
        barrier, inc=1, device_id=(r, c), device_id_type=MESH))

    for load in loads:
        load.wait()
    z, g = z_ref[...], g_ref[...]
    total = g.astype(f32)
    block = wi_ref.shape[1] // rows
    for f in range(rows):
        w_in = wi_ref[:, f * block:(f + 1) * block]
        w_out = wo_ref[f * block:(f + 1) * block, :]
        values, slopes = gelu_parts(dot(z, w_in, 1, 0))
        active = values.astype(bf16)
        grad_hidden = (dot(g, w_out, 1, 1) * slopes).astype(bf16)
        total = total + dot(grad_hidden, w_in, 1, 1)
        part[0, f % 2, f // 2] = dot(z, grad_hidden, 0, 0).astype(bf16)
        part[1, f % 2, f // 2] = dot(active, g, 0, 0).astype(bf16)
        if f == 0:
            x_send[...] = x_ref[...].astype(f32).T.reshape(n, own, pixels).astype(bf16)
            x_recv[pl.ds(me, 1)] = x_send[pl.ds(me, 1)]
            pl.semaphore_wait(barrier, n - 1)
            to_all(lambda t, r, c: send(x_send.at[t], x_recv.at[me], 0, r, c))
    g_send[...] = total.T.reshape(n, own, pixels).astype(bf16)
    g_recv[pl.ds(me, 1)] = g_send[pl.ds(me, 1)]
    to_all(lambda t, r, c: send(g_send.at[t], g_recv.at[me], 1, r, c))
    for s in range(2):
        send(part.at[s, other], from_pair.at[s], 4 + s, my_row + other - core, my_col)

    taps[...] = jnp.zeros_like(taps)
    for a in range(side):
        tap = k_ref[a].astype(f32)
        at = lead + tile_cols * a
        taps[0, at:at + radius + 1, :] = tap[radius:]
        taps[1, at + tile_cols - radius:at + tile_cols, :] = tap[:radius]
    lanes_at = pl.multiple_of(me * own // LANE * LANE, LANE)
    for sign in range(2):
        taps_t[...] = taps[sign, :, pl.ds(lanes_at, LANE)].T
        line = taps_t[pl.ds(pl.multiple_of(lax.rem(me * own, LANE), SUB), own), :]
        for t in range(SUB):
            skew[sign * own:(sign + 1) * own, t, :] = pltpu.roll(line, t, 1) if t else line

    at_or_after = (
        lax.broadcasted_iota(jnp.int32, (tile_cols, span), 1) % tile_cols
        >= lax.broadcasted_iota(jnp.int32, (tile_cols, span), 0)
    )
    offsets = (-1, 0, 1)

    def window(q_first, q_last):
        low = (lead + q_first * tile_cols) // LANE * LANE
        high = round_up(lead + (q_last + 1) * tile_cols - 1 + side * tile_cols, LANE)
        return low, min(high, span)

    tile = lax.broadcasted_iota(jnp.int32, (n, pixels), 0) % cols
    inner[0] = jnp.where(tile > 0, 1.0, 0.0)
    inner[1] = jnp.where(tile < cols - 1, 1.0, 0.0)

    def aside(v, d_col):
        if d_col == 0:
            return v
        return roll_left(v, d_col, 0) * inner[0 if d_col < 0 else 1]


    sum_pair()
    bytes_of(x_recv.at[pl.ds(0, n - 1)], rsem.at[0])
    wide[...] = x_recv[...].astype(f32)
    for c in range(own):
        x3[c] = wide[:, c, :]
    bytes_of(g_recv.at[pl.ds(0, n - 1)], rsem.at[1])
    wide[...] = g_recv[...].astype(f32)
    for c in range(own):
        g3[c] = wide[:, c, :]

    def correlate(c):
        here = x3[c]
        for i, d_col in enumerate(offsets):
            beside = aside(here, d_col)
            for j, d_row in enumerate(offsets):
                at = i * span + j * pixels
                x_sh[:, at:at + pixels] = down(beside, -d_row * cols).astype(bf16)
        m_mat[...] = dot(g3[c].astype(bf16), x_sh[...], 0, 0)

        def lagged(q, sign, low, high):
            after, before = ((1, 2), (0, 1))[sign]
            mask = at_or_after[:, :high - low]

            def block_of(q, i):
                return m_mat[
                    q * tile_cols:(q + 1) * tile_cols, i * span + low:i * span + high]

            out = None
            if q >= 1:
                out = jnp.where(mask, block_of(q - 1, after), 0.0)
            if q < chunks:
                more = jnp.where(mask, 0.0, block_of(q, before))
                out = more if out is None else out + more
            return out

        for sign in range(2):
            parts = []
            for i in range(per_block):
                columns = [None] * (width // LANE)
                for q in range(i, chunks + 1, per_block):
                    low, high = window(q, q)
                    v = lagged(q, sign, low, high)
                    first = low // LANE - q // per_block
                    for k in range((high - low) // LANE):
                        u = v[:, k * LANE:(k + 1) * LANE]
                        old = columns[first + k]
                        columns[first + k] = u if old is None else old + u
                blank = jnp.zeros((tile_cols, LANE), f32)
                parts.append(jnp.concatenate(
                    [blank if u is None else u for u in columns], axis=1))
            while len(parts) > 1:
                m = len(parts) // 2
                parts = [parts[i] + roll_left(parts[i + m], m * tile_cols, 1) for i in range(m)]
            v = parts[0]
            m = tile_cols // 2
            while m >= SUB:
                v = v[:m] + roll_left(v[m:], m, 1)
                m //= 2
            folded[sign * own + c] = v

    pl.loop(0, own // 2)(correlate)
    sum_next()
    pl.loop(own // 2, own)(correlate)

    lines = folded[:, 0, :]
    for t in range(1, SUB):
        lines = lines + roll_left(folded[:, t, :], t, 1)
    keep = gk_send.shape[1] // 2
    lines = (lines * scale)[:, :keep]
    gk_send[...] = jnp.concatenate([lines[:own], lines[own:]], axis=1).astype(bf16)
    spot = gk_recv.at[core, my_pair, my_col]
    spot[...] = gk_send[...]
    for p in range(1, cols):
        send(gk_send, spot, 2, my_row, col_at[p])

    sum_last()

    bands[...] = jnp.zeros_like(bands)

    def convolve(c):
        for sign in range(2):
            v = skew[sign * own + c]
            m = SUB
            while m < tile_cols:
                v = jnp.concatenate([v, pltpu.roll(v, m, 1)], axis=0)
                m *= 2
            parts = [v]
            while len(parts) < per_block:
                m = len(parts) * tile_cols
                parts = parts + [pltpu.roll(u, m, 1) for u in parts]
            for i, u in enumerate(parts):
                bands[sign, i * tile_cols:(i + 1) * tile_cols, pixels:pixels + width] = u

        def band(q, sign, low, high):
            at = q % per_block * tile_cols
            skip = pixels - q // per_block * LANE
            return bands[sign, at:at + tile_cols, skip + low:skip + high]

        for q in range(chunks):
            at = slice(q * tile_cols, (q + 1) * tile_cols)
            low, high = window(q, q + 1)
            mask = at_or_after[:, :high - low]
            k_mat[at, low:high] = jnp.where(mask, band(q + 1, 1, low, high), 0.0).astype(bf16)
            k_mat[at, span + low:span + high] = jnp.where(
                mask, band(q + 1, 0, low, high), band(q, 1, low, high)).astype(bf16)
            k_mat[at, 2 * span + low:2 * span + high] = jnp.where(
                mask, 0.0, band(q, 0, low, high)).astype(bf16)
        here = g3[c]
        spread = dot(here.astype(bf16), k_mat[...], 1, 0)
        result = here
        for i, d_col in enumerate(offsets):
            at = i * span
            beside = spread[:, at + pixels:at + 2 * pixels]
            beside = beside + down(spread[:, at:at + pixels], -cols)
            beside = beside + down(spread[:, at + 2 * pixels:at + span], cols)
            result = result + aside(beside, -d_col)
        o3[c] = result

    k_mat[...] = jnp.zeros_like(k_mat)
    pl.loop(0, own // 4)(convolve)
    share_first()
    pl.loop(own // 4, own // 2)(convolve)
    share_next()
    bytes_of(gk_recv.at[0, 0, pl.ds(0, cols - 1)], rsem.at[2])
    spots = gk_recv.at[core, my_pair]
    for p in range(1, pairs):
        send(spots, spots, 16, 2 * lax.rem(my_pair + p, pairs) + core, my_col)
    pl.loop(own // 2, own)(convolve)

    for c in range(own):
        wide[:, c, :] = o3[c]
    o_send[...] = wide[...].astype(bf16)
    o_recv[pl.ds(me, 1)] = o_send[pl.ds(me, 1)]
    to_all(lambda t, r, c: send(o_send.at[t], o_recv.at[me], 3, r, c))

    share_pair()
    bytes_of(gk_recv.at[0, pl.ds(0, pairs - 1)], rsem.at[16])
    send(gk_recv.at[core], gk_recv.at[core], 17, my_row + other - core, my_col)

    bytes_of(o_recv.at[pl.ds(0, n - 1)], rsem.at[3])
    gi_ref[...] = o_recv[...].astype(f32).reshape(channels, pixels).T.astype(bf16)

    bytes_of(gk_recv.at[0], rsem.at[17])
    share = cols * own
    for r in range(rows):
        gk_t[:, r * share:(r + 1) * share] = (
            gk_recv[r % 2, r // 2].astype(f32).reshape(share, 2 * keep).T)
    for a in range(side):
        at = lead + tile_cols * a
        low = gk_t[keep + at + tile_cols - radius:keep + at + tile_cols, :]
        high = gk_t[at:at + radius + 1, :]
        gk_ref[a] = jnp.concatenate([low, high], axis=0).astype(bf16)

    bytes_of(all_b.at[0], rsem.at[15])
    bytes_of(allq.at[0], rsem.at[14])
    for f in range(rows):
        at = slice(f * block, (f + 1) * block)
        gwi_ref[:, at] = allq[f % 2, f // 2].reshape(channels, block)
        for c in range(cols):
            gwo_ref[f * block + c * piece:f * block + (c + 1) * piece, :] = all_b[f % 2, c, f // 2]

    bytes_of(x_send.at[pl.ds(0, n - 1)], ssem.at[0])
    bytes_of(g_send.at[pl.ds(0, n - 1)], ssem.at[1])
    bytes_of(gk_recv.at[0, 0, pl.ds(0, cols - 1)], ssem.at[2])
    bytes_of(gk_recv.at[0, pl.ds(0, pairs - 1)], ssem.at[16])
    bytes_of(gk_recv.at[0], ssem.at[17])
    bytes_of(o_send.at[pl.ds(0, n - 1)], ssem.at[3])
    for s in range(2):
        bytes_of(from_pair.at[s], ssem.at[4 + s])
    bytes_of(paired.at[0, pl.ds(0, pairs - 1)], ssem.at[6])
    bytes_of(paired_b.at[pl.ds(0, cols - 1)], ssem.at[7])
    bytes_of(half.at[pl.ds(0, cols - 1)], ssem.at[8])
    bytes_of(half_b.at[pl.ds(0, pairs - 1)], ssem.at[9])
    bytes_of(half.at[pl.ds(0, cols - 1)], ssem.at[10])
    bytes_of(half_b.at[pl.ds(0, pairs - 1)], ssem.at[11])
    bytes_of(allq.at[0, pl.ds(0, pairs - 1)], ssem.at[12])
    bytes_of(all_b.at[0, pl.ds(0, cols - 1)], ssem.at[13])
    bytes_of(allq.at[0], ssem.at[14])
    bytes_of(all_b.at[0], ssem.at[15])


def hand_over_kernel(count, *refs):
    ins, outs, held, sems = refs[:count], refs[count:2 * count], refs[2 * count:-1], refs[-1]
    first = [pltpu.make_async_copy(ins[i], held[i], sems.at[0, i]) for i in range(count)]
    then = [pltpu.make_async_copy(held[i], outs[i], sems.at[1, i]) for i in range(count)]
    for copy in first:
        copy.start()
    for i in range(count):
        first[i].wait()
        then[i].start()
    for copy in then:
        copy.wait()


def fits(rows, cols, tile_rows, tile_cols, channels, hidden):
    n = rows * cols
    pixels = tile_rows * tile_cols
    radius = KS // 2
    return (
        channels % n == 0
        and channels // n == SUB
        and channels % LANE == 0
        and rows % 2 == 0
        and rows > 2
        and cols % 2 == 0
        and hidden == rows * channels
        and pixels == 2 * LANE
        and tile_cols == 2 * SUB
        and radius < min(tile_rows, tile_cols)
        and channels % (cols * 2 * SUB) == 0
    )


def fused_device(inputs, stored, upstream, weight_in, weight_out, kernel):
    rows, cols = lax.axis_size("row"), lax.axis_size("col")
    tile_rows, tile_cols, channels = stored.shape
    n, pixels, hidden = rows * cols, tile_rows * tile_cols, weight_in.shape[1]
    side = kernel.shape[0]
    radius = side // 2
    own = channels // n
    taps = pixels - tile_cols * radius - tile_cols + tile_cols * side
    width = round_up(taps + LANE - 1, LANE)
    keep = round_up(taps, LANE)
    span = 3 * pixels
    scale = 1.0 / math.sqrt(pixels * n)
    bf16, f32 = jnp.bfloat16, jnp.float32
    flat = (pixels, channels)
    piece = channels // cols
    pairs = rows // 2
    vmem = pl.BlockSpec(memory_space=pltpu.VMEM)
    results = pl.pallas_call(
        lambda *refs: fused_kernel(rows, cols, tile_cols, radius, scale, *refs),
        out_shape=(
            jax.ShapeDtypeStruct(flat, bf16),
            jax.ShapeDtypeStruct(weight_in.shape, bf16),
            jax.ShapeDtypeStruct(weight_out.shape, bf16),
            jax.ShapeDtypeStruct(kernel.shape, bf16),
        ),
        in_specs=[pl.BlockSpec(memory_space=pltpu.HBM)] * 6,
        out_specs=(vmem,) * 4,
        scratch_shapes=[pltpu.VMEM(flat, bf16)] * 3 + [
            pltpu.VMEM(weight_in.shape, bf16),
            pltpu.VMEM(weight_out.shape, bf16),
            pltpu.VMEM(kernel.shape, bf16),
        ] + [pltpu.VMEM((n, own, pixels), bf16)] * 6 + [
            pltpu.VMEM((2, 2, pairs, channels, channels), bf16),
            pltpu.VMEM((2, pairs, channels, channels), bf16),
            pltpu.VMEM((1, pairs, channels, channels), bf16),
            pltpu.VMEM((pairs, channels, channels), bf16),
            pltpu.VMEM((cols, piece, channels), bf16),
            pltpu.VMEM((cols, piece, channels), bf16),
            pltpu.VMEM((2, pairs, cols, piece, channels), bf16),
            pltpu.VMEM((cols, pairs, piece, channels), bf16),
            pltpu.VMEM((cols, pairs, piece, channels), bf16),
            pltpu.VMEM((pairs, piece, channels), bf16),
            pltpu.VMEM((pairs, piece, channels), bf16),
            pltpu.VMEM((2, cols, pairs, piece, channels), bf16),
            pltpu.VMEM((own, 2 * keep), bf16),
            pltpu.VMEM((2, pairs, cols, own, 2 * keep), bf16),
            pltpu.VMEM((n, own, pixels), f32),
            pltpu.VMEM((own, n, pixels), f32),
            pltpu.VMEM((own, n, pixels), f32),
            pltpu.VMEM((own, n, pixels), f32),
            pltpu.VMEM((2, width, channels), f32),
            pltpu.VMEM((LANE, width), f32),
            pltpu.VMEM((2 * own, SUB, width), f32),
            pltpu.VMEM((2 * own, SUB, width), f32),
            pltpu.VMEM((2, LANE, pixels + span), f32),
            pltpu.VMEM((pixels, 3 * span), bf16),
            pltpu.VMEM((pixels, 3 * span), f32),
            pltpu.VMEM((n, 3 * span), bf16),
            pltpu.VMEM((2 * keep, channels), f32),
            pltpu.VMEM((2, n, pixels), f32),
            pltpu.SemaphoreType.DMA((6,)),
            pltpu.SemaphoreType.DMA((18,)),
            pltpu.SemaphoreType.DMA((18,)),
        ],
        compiler_params=pltpu.CompilerParams(
            collective_id=0, has_side_effects=True, vmem_limit_bytes=64 * 1024 * 1024
        ),
    )(
        inputs.reshape(flat), stored.reshape(flat), upstream.reshape(flat),
        weight_in, weight_out, kernel,
    )
    results = pl.pallas_call(
        lambda *refs: hand_over_kernel(len(results), *refs),
        out_shape=tuple(jax.ShapeDtypeStruct(r.shape, r.dtype) for r in results),
        in_specs=[pl.BlockSpec(memory_space=pl.ANY)] * len(results),
        out_specs=(pl.BlockSpec(memory_space=pl.ANY),) * len(results),
        scratch_shapes=[pltpu.VMEM(r.shape, r.dtype) for r in results]
        + [pltpu.SemaphoreType.DMA((2, len(results)))],
        compiler_params=pltpu.CompilerParams(vmem_limit_bytes=64 * 1024 * 1024),
    )(*results)
    return (results[0].reshape(stored.shape), *results[1:])


def per_device(inputs, stored, upstream, weight_in, weight_out, kernel):
    args = (inputs, stored, upstream, weight_in, weight_out, kernel)
    sizes = (lax.axis_size("row"), lax.axis_size("col"))
    if fits(*sizes, *stored.shape, weight_in.shape[1]):
        return fused_device(*args)
    return sweep_device(*args)


def solution(mesh):
    return jax.shard_map(
        per_device,
        mesh=mesh,
        in_specs=(
            P("row", "col", None),
            P("row", "col", None),
            P("row", "col", None),
            P(),
            P(),
            P(),
        ),
        out_specs=(P("row", "col", None), P(), P(), P()),
        check_vma=False,
    )
```
